32 devices in a mesh: tm: 16 (over z, y, x), inp: 2 (over core).
Axes of the slice: x: 2, y: 2, z: 4, core: 2. Of those that a mesh axis runs over, the one named last changes fastest.
Arguments:
- voltages: bfloat16 [2, 65536, 1024], P(None, 'tm', 'inp'), may hold values from -127 to 127, as said below
- taps: int32 [12, 1024], replicated, may hold values from -64 to 64
Outputs:
- visibility: bfloat16 [512, 1024, 1024], P(('tm', 'inp'))
The draws below stay inside these ranges and needn't reach their ends.
Inputs may be any that keep to these rules, and one draw needn't show every extreme that they name: `voltages`: every sample is a whole number.
All inputs are finite; a program needn't handle non-finite values.
Results may differ from the reference program's by a relative error of at most 0.0048.
Values may be sent and summed in bfloat16 or wider, within the bound.
No kernel may reach another device: no remote copies, remote signals or barrier semaphores. Data moves between devices by JAX's collectives and lax.ppermute only.
A program may use at most 576 MiB of HBM per device.

```python
import math
import jax
import jax.numpy as jnp
from jax import lax

INPUTS = 1024
FINE = 1024
KEEP = 512
TAPS = 12
NSPEC = 64
SAMPLES = 65536


def draw_voltages(key, part):
    base_key = jax.random.fold_in(key, 7)
    key_list = jax.random.split(base_key, 4)
    amplitude = jax.random.randint(key_list[0], (1, 1, INPUTS), 16, 96)
    noise_part = jax.random.randint(key_list[1], (2, SAMPLES, INPUTS), -amplitude, amplitude + 1)
    sky_signal = jax.random.randint(key_list[2], (2, SAMPLES, 1), -16, 17)
    sky_weight = jax.random.randint(key_list[3], (1, 1, INPUTS), -2, 3)
    return (noise_part + sky_weight * sky_signal).astype(jnp.float32).astype(jnp.bfloat16)


def touch_ends(drawn, key, smallest, top_value):
    shape = drawn.shape
    spot = [jax.random.randint(jax.random.fold_in(key, axis), (), 0, shape[axis]) for axis in range(len(shape))]
    drawn = drawn.at[tuple(spot)].set(smallest)
    longest = shape.index(max(shape))
    spot[longest] = (spot[longest] + 1) % shape[longest]
    return drawn.at[tuple(spot)].set(top_value)


def setup_inputs(seed: int = 0) -> dict:
    splits = jax.random.split(jax.random.key(seed), 3)
    voltages = draw_voltages(jax.random.fold_in(splits[2], 71), 0)
    taps = touch_ends(jax.random.randint(splits[1], (TAPS, FINE), -64, 65), jax.random.fold_in(splits[1], 1), -64, 64).astype(jnp.int32)
    return dict(voltages=voltages, taps=taps)


def dft_table(fine_count, keep_count):
    branch = jnp.arange(fine_count, dtype=jnp.int32)[:, None]
    channel = jnp.arange(keep_count, dtype=jnp.int32)[None, :] - keep_count // 2
    phase_index = jnp.mod(branch * channel, fine_count).astype(jnp.float32)
    angles = 2.0 * math.pi / fine_count * phase_index
    norm_scale = 1.0 / math.sqrt(fine_count)
    cosine = jnp.cos(angles) * norm_scale
    sine_part = jnp.sin(angles) * norm_scale
    dft_matrix = jnp.stack([jnp.stack([cosine, -sine_part], 1), jnp.stack([sine_part, cosine], 1)], 0)
    return dft_matrix.astype(jnp.bfloat16)

def reference(voltages, taps):
    history_len = TAPS - 1
    dft_matrix = dft_table(FINE, KEEP).astype(jnp.float32)
    coefficient = taps.astype(jnp.float32)
    block_count = max(INPUTS // 128, 1)
    block_width = INPUTS // block_count
    volt_blocks = voltages.reshape(2, NSPEC, FINE, block_count, block_width).transpose(3, 0, 1, 2, 4)

    def spectra_of(volt_block):
        padded = jnp.pad(volt_block.astype(jnp.float32), ((0, 0), (history_len, 0), (0, 0), (0, 0)))
        filtered = jnp.zeros((2, NSPEC, FINE, block_width), jnp.float32)
        for k in range(TAPS):
            filtered = filtered + coefficient[k][None, None, :, None] * padded[:, history_len - k:history_len - k + NSPEC]
        filtered = (filtered * (1.0 / 8192.0)).astype(jnp.bfloat16)
        spectra_block = jnp.einsum('rfna,rnsj->jsfa', filtered.astype(jnp.float32), dft_matrix)
        return spectra_block.astype(jnp.bfloat16)
    channel_spectra = lax.map(spectra_of, volt_blocks)
    channel_spectra = channel_spectra.transpose(1, 2, 3, 0, 4).reshape(KEEP, 2, NSPEC, INPUTS)
    upper_mask = jnp.arange(INPUTS)[:, None] <= jnp.arange(INPUTS)[None, :]

    def correlate(spectra_one):
        stacked_rows = spectra_one.reshape(2 * NSPEC, INPUTS)
        turned = jnp.concatenate([-spectra_one[1], spectra_one[0]], 0)
        real_part = jnp.dot(stacked_rows.T, stacked_rows, preferred_element_type=jnp.float32)
        imag_part = jnp.dot(stacked_rows.T, turned, preferred_element_type=jnp.float32)
        norm_scale = 1.0 / NSPEC
        return jnp.where(upper_mask, real_part * norm_scale, imag_part * norm_scale).astype(jnp.bfloat16)
    return lax.map(correlate, channel_spectra)
```

```python
import functools
import math

import jax
import jax.numpy as jnp
import numpy as np
from jax import lax
from jax.experimental import pallas as pl
from jax.experimental.pallas import tpu as pltpu
from jax.sharding import PartitionSpec as P

KEEP = 512
RADIX = 4
MIB = 1 << 20


def dft_tables(fine, keep):
    base = fine // RADIX
    branch = np.arange(base)[None, :]
    channel = np.arange(keep)[:, None]
    phase = np.mod(branch * (channel - keep // 2), fine)
    angle = 2.0 * np.pi / fine * phase
    norm = 1.0 / math.sqrt(fine)
    both = np.stack([np.cos(angle) * norm, -np.sin(angle) * norm])
    both = both.reshape(2, keep // RADIX, RADIX, base).transpose(2, 0, 1, 3)
    return both.reshape(RADIX, 2 * (keep // RADIX), base).astype(np.float32)


def pack_kernel(peers, half, place, *refs):
    ins, outs = refs[:peers], refs[peers:]
    for k in range(peers):
        real = ins[k][0].astype(jnp.float32)
        imag = ins[k][1].astype(jnp.float32)
        low = lax.broadcasted_iota(jnp.int32, real.shape, 1) < half
        outs[k][...] = jnp.where(low, real, pltpu.roll(imag, half, 1)).astype(jnp.bfloat16)
        outs[peers + k][...] = jnp.where(low, pltpu.roll(real, half, 1), imag).astype(jnp.bfloat16)


def pack(voltages, place, peers):
    rows, width = voltages.shape[1:]
    lanes = width // peers
    step = min(rows, 512)
    spec = [
        pl.BlockSpec((2, step, lanes), functools.partial(lambda k, i, p: (0, i, jnp.bitwise_xor(p[0], k)), k))
        for k in range(peers)
    ]
    out_spec = [pl.BlockSpec((step, lanes), lambda i, p: (i, 0))] * (2 * peers)
    return pl.pallas_call(
        functools.partial(pack_kernel, peers, lanes // 2),
        grid_spec=pltpu.PrefetchScalarGridSpec(
            num_scalar_prefetch=1, grid=(rows // step,), in_specs=spec, out_specs=out_spec
        ),
        out_shape=[jax.ShapeDtypeStruct((rows, lanes), jnp.bfloat16)] * (2 * peers),
        compiler_params=pltpu.CompilerParams(vmem_limit_bytes=40 * MIB),
        name="pack",
    )(place, *([voltages] * peers))


def spectra_kernel(dims, place, *refs):
    peers, frames, taps_n, base, per_res, dests, chan, tail_step, step = dims
    pieces = refs[:peers]
    taps, table, out, xs, ys, zs, heads, tails = refs[peers:]
    own = peers * frames
    past = taps_n - 1
    total = own + past
    lanes = xs.shape[-1]
    half = lanes // 2
    at = pl.program_id(0)

    for k in range(peers):
        first = jnp.bitwise_xor(place[0], k) * frames
        for f in range(frames):
            xs[first + f] = pieces[k][f].astype(jnp.float32)

    flip = jnp.where(lax.broadcasted_iota(jnp.int32, (16, lanes), 1) < half, 1.0, -1.0)

    @pl.when(at == 0)
    def _():
        for c in range(RADIX):
            zs[c, (total + 1) // 2 - 1] = jnp.zeros(zs.shape[2:], zs.dtype)

    def filter_rows(b, carry):
        row = pl.multiple_of(b * 16, 16)
        for q in range(RADIX):
            for s in range(2):
                here = pl.ds(pl.multiple_of(row + 8 * s, 8), 8)
                weight = taps[q, pl.ds(pl.multiple_of(at * step + row + 8 * s, 8), 8), :]
                weights = [jnp.broadcast_to(weight[:, k : k + 1], (8, lanes)) for k in range(taps_n)]
                x = [xs[f, q, here, :] for f in range(own)]
                for f in range(total):
                    parts = [weights[k] * x[f - k] for k in range(taps_n) if 0 <= f - k < own]
                    while len(parts) > 1:
                        parts = [sum(parts[i : i + 2]) for i in range(0, len(parts), 2)]
                    ys[q, f, pl.ds(8 * s, 8), :] = parts[0]
        place_rows = pl.ds(pl.multiple_of(at * step + row, 16), 16)
        for f in range(total):
            y0, y1, y2, y3 = (ys[q, f] for q in range(RADIX))
            even, odd = y0 + y2, y1 + y3
            diff = y0 - y2
            turned = pltpu.roll(y1 - y3, half, 1) * flip
            side = pl.ds((f % 2) * lanes, lanes)
            for c, value in enumerate((even + odd, diff + turned, even - odd, diff - turned)):
                zs[c, f // 2, place_rows, side] = value.astype(jnp.bfloat16)
        return carry

    lax.fori_loop(0, step // 16, filter_rows, 0)

    @pl.when(at == pl.num_programs(0) - 1)
    def _():
        sign = jnp.where(lax.broadcasted_iota(jnp.int32, (per_res, lanes), 1) < half, -1.0, 1.0)

        def transform(pair, c):
            both = jnp.dot(table[c], zs[c, pair], preferred_element_type=jnp.float32)
            return [
                both[:per_res, u * lanes : (u + 1) * lanes]
                + pltpu.roll(both[per_res:, u * lanes : (u + 1) * lanes], half, 1) * sign
                for u in range(2)
            ]

        def head_pair(pair, carry):
            for c in range(RADIX):
                for u, value in enumerate(transform(pair, c)):
                    heads[pl.ds(c * own + pair * 2 + u, per_res, stride=RADIX * own), :] = value
            return carry

        lax.fori_loop(0, own // 2, head_pair, 0)
        for pair in range(own // 2, (total + 1) // 2):
            for c in range(RADIX):
                for u, value in enumerate(transform(pair, c)):
                    f = pair * 2 + u - own
                    if f < past:
                        tails[pl.ds(c * past + f, per_res, stride=tail_step), :] = value
        head_rows = chan * own
        tail_rows = chan // RADIX * tail_step

        def emit(d, carry):
            out[d, pl.ds(0, head_rows), :] = heads[
                pl.ds(pl.multiple_of(d * head_rows, 16), head_rows), :
            ].astype(jnp.bfloat16)
            out[d, pl.ds(head_rows, tail_rows), :] = tails[
                pl.ds(pl.multiple_of(d * tail_rows, 16), tail_rows), :
            ].astype(jnp.bfloat16)
            return carry

        lax.fori_loop(0, dests, emit, 0)


def tail_stride(chan, past):
    stride = RADIX * past
    if chan // RADIX * stride % 16:
        stride = -(-stride // 16) * 16
    return stride


def spectra(pieces, place, taps, table, frames, dests, chan):
    peers = len(pieces)
    lanes = pieces[0].shape[-1]
    fine, taps_n = taps.shape[1], taps.shape[0]
    base = fine // RADIX
    keep = chan * dests
    per_res = keep // RADIX
    own, past = peers * frames, taps_n - 1
    pairs = (own + past + 1) // 2
    stride = tail_stride(chan, past)
    step = min(base, 64)
    dims = (peers, frames, taps_n, base, per_res, dests, chan, stride, step)
    rows = chan * own + chan // RADIX * stride
    weights = (taps.astype(jnp.float32) * (1.0 / 8192.0)).T.reshape(RADIX, base, taps_n)
    blocks = [piece.reshape(frames, RADIX, base, lanes) for piece in pieces]
    whole = lambda shape: pl.BlockSpec(shape, lambda i, p: (0,) * len(shape))
    return pl.pallas_call(
        functools.partial(spectra_kernel, dims),
        grid_spec=pltpu.PrefetchScalarGridSpec(
            num_scalar_prefetch=1,
            grid=(base // step,),
            in_specs=[pl.BlockSpec((frames, RADIX, step, lanes), lambda i, p: (0, 0, i, 0))] * peers
            + [whole(weights.shape), whole(table.shape)],
            out_specs=whole((dests, rows, lanes)),
            scratch_shapes=[
                pltpu.VMEM((own, RADIX, step, lanes), jnp.float32),
                pltpu.VMEM((RADIX, own + past, 16, lanes), jnp.float32),
                pltpu.VMEM((RADIX, pairs, base, 2 * lanes), jnp.bfloat16),
                pltpu.VMEM((keep * own, lanes), jnp.float32),
                pltpu.VMEM((per_res * stride, lanes), jnp.float32),
            ],
        ),
        out_shape=jax.ShapeDtypeStruct((dests, rows, lanes), jnp.bfloat16),
        compiler_params=pltpu.CompilerParams(vmem_limit_bytes=56 * MIB),
        name="spectra",
    )(place, *blocks, weights, table)


def gram_kernel(dims, first, second, out, tails, stacked, turned):
    planes, peers, cores, own, past, chan, stride, scale = dims
    lanes = first.shape[-1]
    half = lanes // 2
    ch = pl.program_id(0)
    head_rows = chan * own
    tail_rows = chan // RADIX * stride
    sources = planes * peers * cores
    inputs = peers * cores * lanes
    depth = planes * own

    @pl.when(ch == 0)
    def _():
        def widen(d, carry):
            for h, ref in enumerate((first, second)):
                tails[h, d, pl.ds(0, tail_rows), :] = ref[d, pl.ds(head_rows, tail_rows), :].astype(jnp.float32)
                tails[h, d, pl.ds(tail_rows, 16), :] = jnp.zeros((16, lanes), jnp.float32)
            return carry

        lax.fori_loop(0, sources, widen, 0)

    low = lax.broadcasted_iota(jnp.int32, (own, lanes), 1) < half
    early = lax.broadcasted_iota(jnp.int32, (own, lanes), 0) < past
    tail_at = ch // RADIX * stride + ch % RADIX * past
    head_at = pl.multiple_of(ch * own, 16)
    for z in range(planes):
        for q in range(peers):
            for c in range(cores):
                source = (z * peers + q) * cores + c
                value = []
                for h, ref in enumerate((first, second)):
                    v = ref[source, pl.ds(head_at, own), :].astype(jnp.float32)
                    if z:
                        late = tails[h, source - peers * cores, pl.ds(tail_at, own), :]
                        v = v + jnp.where(early, late, 0.0)
                    value.append(v)
                a, b = value
                real = jnp.where(low, a, pltpu.roll(b, half, 1)).astype(jnp.bfloat16)
                imag = jnp.where(low, pltpu.roll(a, half, 1), b)
                column = pl.ds((c * peers + q) * lanes, lanes)
                stacked[pl.ds(z * own, own), column] = real
                stacked[pl.ds(depth + z * own, own), column] = imag.astype(jnp.bfloat16)
                turned[pl.ds(z * own, own), column] = (-imag).astype(jnp.bfloat16)
                turned[pl.ds(depth + z * own, own), column] = real

    block = min(256, inputs)
    diagonal = (
        lax.broadcasted_iota(jnp.int32, (block, block), 0) <= lax.broadcasted_iota(jnp.int32, (block, block), 1)
    )
    for i in range(inputs // block):
        left = stacked[:, i * block : (i + 1) * block].T

        def product(ref, lo, hi):
            return jnp.dot(left, ref[:, lo:hi], preferred_element_type=jnp.float32) * scale

        rows = pl.ds(i * block, block)
        lo, hi = i * block, (i + 1) * block
        if lo:
            out[0, rows, 0:lo] = product(turned, 0, lo).astype(jnp.bfloat16)
        mixed = jnp.where(diagonal, product(stacked, lo, hi), product(turned, lo, hi))
        out[0, rows, lo:hi] = mixed.astype(jnp.bfloat16)
        if hi < inputs:
            out[0, rows, hi:inputs] = product(stacked, hi, inputs).astype(jnp.bfloat16)


def gram(first, second, planes, peers, cores, own, past, chan, scale):
    sources, rows, lanes = first.shape
    inputs = peers * cores * lanes
    stride = tail_stride(chan, past)
    tail_rows = chan // RADIX * stride
    depth = planes * own
    whole = pl.BlockSpec(first.shape, lambda i: (0, 0, 0))
    dims = (planes, peers, cores, own, past, chan, stride, scale)
    return pl.pallas_call(
        functools.partial(gram_kernel, dims),
        grid=(chan,),
        in_specs=[whole, whole],
        out_specs=pl.BlockSpec((1, inputs, inputs), lambda i: (i, 0, 0)),
        scratch_shapes=[
            pltpu.VMEM((2, sources, tail_rows + 16, lanes), jnp.float32),
            pltpu.VMEM((2 * depth, inputs), jnp.bfloat16),
            pltpu.VMEM((2 * depth, inputs), jnp.bfloat16),
        ],
        out_shape=jax.ShapeDtypeStruct((chan, inputs, inputs), jnp.bfloat16),
        compiler_params=pltpu.CompilerParams(vmem_limit_bytes=56 * MIB),
        name="gram",
    )(first, second)


def per_device(voltages, taps):
    past, fine = taps.shape[0] - 1, taps.shape[1]
    frames = voltages.shape[1] // fine
    n_time, n_group = lax.axis_size("tm"), lax.axis_size("inp")
    dests = n_time * n_group
    chan = KEEP // dests
    peers = 1
    while peers * frames < past:
        peers *= 2
    planes = n_time // peers
    own = peers * frames
    place = jnp.bitwise_and(lax.axis_index("tm"), peers - 1).astype(jnp.int32)[None]
    table = jnp.asarray(dft_tables(fine, KEEP).astype(jnp.bfloat16))

    packed = pack(voltages, place, peers)
    halves = [packed[:peers], packed[peers:]]
    turned = []
    for h in range(2):
        pieces = halves[h]
        if h:
            pieces, turned[0] = lax.optimization_barrier((pieces, turned[0]))
        moved = [pieces[0]]
        for k in range(1, peers):
            moved.append(lax.ppermute(pieces[k], "tm", [(t, t ^ k) for t in range(n_time)]))
        turned.append(moved)
    received = []
    for h in range(2):
        mine = spectra(turned[h], place, taps, table, frames, dests, chan)
        received.append(lax.all_to_all(mine, ("tm", "inp"), split_axis=0, concat_axis=0, tiled=True))
    return gram(*received, planes, peers, n_group, own, past, chan, 1.0 / (n_time * frames))


def solution(mesh):
    return jax.shard_map(
        per_device,
        mesh=mesh,
        in_specs=(P(None, "tm", "inp"), P()),
        out_specs=P(("tm", "inp"), None, None),
        check_vma=False,
    )
```

```python
import functools
import math

import jax
import jax.numpy as jnp
import numpy as np
from jax import lax
from jax.experimental import pallas as pl
from jax.experimental.pallas import tpu as pltpu
from jax.sharding import PartitionSpec as P

KEEP = 512
RADIX = 4
LANES = 128
PEERS = 4
SUB = LANES // PEERS
MIB = 1 << 20


def dft_tables(fine, keep):
    base = fine // RADIX
    branch = np.arange(base)[None, :]
    channel = np.arange(keep)[:, None]
    phase = np.mod(branch * (channel - keep // 2), fine)
    angle = 2.0 * np.pi / fine * phase
    norm = 1.0 / math.sqrt(fine)
    cosine = (np.cos(angle) * norm).reshape(keep // RADIX, RADIX, base)
    sine = (-np.sin(angle) * norm).reshape(keep // RADIX, RADIX, base)
    plain = np.stack([np.concatenate([cosine[:, c], sine[:, c]]) for c in (0, 2)])
    odd = [
        np.block([[cosine[:, c], sign * sine[:, c]], [sine[:, c], -sign * cosine[:, c]]])
        for c, sign in ((1, 1.0), (3, -1.0))
    ]
    return plain.astype(np.float32), np.concatenate(odd).astype(np.float32)


def lane(shape):
    return lax.broadcasted_iota(jnp.int32, shape, len(shape) - 1)


def blocks_transposed(x):
    low = lane(x[0].shape) < 2 * SUB
    even = lane(x[0].shape) % (2 * SUB) < SUB
    mid = [None] * 4
    for i in range(2):
        a, b = x[i], x[i + 2]
        mid[i] = jnp.where(low, a, pltpu.roll(b, 2 * SUB, 1))
        mid[i + 2] = jnp.where(low, pltpu.roll(a, 2 * SUB, 1), b)
    out = []
    for i in (0, 2):
        a, b = mid[i], mid[i + 1]
        out.append(jnp.where(even, a, pltpu.roll(b, SUB, 1)))
        out.append(jnp.where(even, pltpu.roll(a, LANES - SUB, 1), b))
    return out


def pack_kernel(place, source, *refs):
    outs, select = refs[:PEERS], refs[PEERS]

    @pl.when(pl.program_id(0) == 0)
    def _():
        shape = select.shape
        row, column = (lax.broadcasted_iota(jnp.int32, shape, axis) for axis in range(2))
        peer = jnp.bitwise_xor(column // LANES, place[0])
        wanted = (column % LANES) // SUB * LANES + peer * SUB + column % SUB
        select[...] = jnp.where(row == wanted, 1.0, 0.0).astype(jnp.bfloat16)

    x = jnp.concatenate([source[r, 0, upper] for upper in range(2) for r in range(2)], 1)
    moved = jnp.dot(x, select[...], preferred_element_type=jnp.float32).astype(jnp.bfloat16)
    for k in range(PEERS):
        outs[k][...] = moved[:, k * LANES : (k + 1) * LANES]


def pack(voltages, place, chunk, fine):
    frames = voltages.shape[1] // fine
    rows = fine // 2
    shaped = voltages.reshape(2, frames, 2, rows, voltages.shape[2])
    return pl.pallas_call(
        pack_kernel,
        grid_spec=pltpu.PrefetchScalarGridSpec(
            num_scalar_prefetch=1,
            grid=(frames,),
            in_specs=[pl.BlockSpec((2, 1, 2, rows, LANES), lambda i, p: (0, i, 0, 0, chunk))],
            out_specs=[pl.BlockSpec((rows, LANES), lambda i, p: (i, 0))] * PEERS,
            scratch_shapes=[pltpu.VMEM((PEERS * LANES, PEERS * LANES), jnp.bfloat16)],
        ),
        out_shape=[jax.ShapeDtypeStruct((frames * rows, LANES), jnp.bfloat16)] * PEERS,
        compiler_params=pltpu.CompilerParams(vmem_limit_bytes=40 * MIB),
        name="pack",
    )(place, shaped)


def spectra_kernel(dims, place, *refs):
    frames, taps_n, base, per_res, dests, chan, head_rows, tail_rows, step = dims
    pieces = refs[:PEERS]
    taps, plain, odd = refs[PEERS : PEERS + 3]
    out, xs, ys, zs, heads, tails = refs[-6:]
    own = PEERS * frames
    past = taps_n - 1
    total = own + past
    half = LANES // 2
    head_pairs, tail_pairs = own // 2, (past + 1) // 2
    pitch = heads.shape[0] // (per_res * RADIX)
    at = pl.program_id(0)

    for k in range(PEERS):
        first = jnp.bitwise_xor(place[0], k) * frames
        for f in range(frames):
            xs[first + f] = pieces[k][f].astype(jnp.float32)

    low = lane((8, LANES)) < half
    low16 = lane((16, LANES)) < half
    flip = jnp.where(low16, 1.0, -1.0)

    if total % 2:

        @pl.when(at == 0)
        def _():
            ys[:, total] = jnp.zeros(ys.shape[:1] + ys.shape[2:], ys.dtype)

    def filter_rows(b, carry):
        row = pl.multiple_of(b * 16, 16)
        for q in range(2):
            for s in range(2):
                here = pl.ds(pl.multiple_of(row + 8 * s, 8), 8)
                weight = taps[q, pl.ds(pl.multiple_of(at * step + row + 8 * s, 8), 8), :]
                wide = [jnp.broadcast_to(weight[:, k : k + 1], (8, LANES)) for k in range(2 * taps_n)]
                weights = [jnp.where(low, wide[k], wide[k + taps_n]) for k in range(taps_n)]
                x = [xs[f, q, here, :] for f in range(own)]
                for f in range(total):
                    parts = [weights[k] * x[f - k] for k in range(taps_n) if 0 <= f - k < own]
                    while len(parts) > 1:
                        parts = [sum(parts[i : i + 2]) for i in range(0, len(parts), 2)]
                    ys[q, f, pl.ds(8 * s, 8), :] = parts[0]
        for pair in range(head_pairs + tail_pairs):

            def sum_and_difference(q):
                first, second = ys[q, 2 * pair], ys[q, 2 * pair + 1]
                kept = jnp.where(low16, first, second)
                other = pltpu.roll(jnp.where(low16, second, first), half, 1)
                return kept + other, (kept - other) * flip

            a_sum, a_diff = sum_and_difference(0)
            b_sum, b_diff = sum_and_difference(1)
            side = pl.ds((pair % 2) * LANES, LANES)
            for part, value in enumerate((a_sum + b_sum, a_sum - b_sum, a_diff, b_diff)):
                rows = pl.ds(pl.multiple_of(part * base + at * step + row, 16), 16)
                zs[pair // 2, rows, side] = value.astype(jnp.bfloat16)
        return carry

    lax.fori_loop(0, step // 16, filter_rows, 0)

    @pl.when(at == pl.num_programs(0) - 1)
    def _():
        even = lane((per_res, LANES)) % (2 * SUB) < SUB

        def keep(quad, c, both):
            for u in range(2):
                sine = both[per_res:, u * LANES : (u + 1) * LANES]
                turned = jnp.where(even, -pltpu.roll(sine, LANES - SUB, 1), pltpu.roll(sine, SUB, 1))
                value = both[:per_res, u * LANES : (u + 1) * LANES] + turned
                pair = quad * 2 + u
                if pair < head_pairs:
                    heads[pl.ds(c * pitch + pair, per_res, stride=RADIX * pitch), :] = value
                elif pair < head_pairs + tail_pairs:
                    tails[pl.ds(c * tail_pairs + pair - head_pairs, per_res, stride=RADIX * tail_pairs), :] = value

        for quad in range((head_pairs + tail_pairs + 1) // 2):
            for i in range(2):
                rows = zs[quad, i * base : (i + 1) * base]
                keep(quad, 2 * i, jnp.dot(plain[i], rows, preferred_element_type=jnp.float32))
            both = jnp.dot(odd[...], zs[quad, 2 * base :], preferred_element_type=jnp.float32)
            keep(quad, 1, both[: 2 * per_res])
            keep(quad, 3, both[2 * per_res :])

        def emit(d, carry):
            for e in range(0, chan, 16 // head_pairs):
                rows = [heads[pl.ds((d * chan + e + i) * pitch, head_pairs), :] for i in range(16 // head_pairs)]
                out[d, pl.ds(e * head_pairs, 16), :] = jnp.concatenate(rows, 0).astype(jnp.bfloat16)
            out[d, pl.ds(head_rows, tail_rows), :] = tails[
                pl.ds(pl.multiple_of(d * chan * tail_pairs, 8), tail_rows), :
            ].astype(jnp.bfloat16)
            return carry

        lax.fori_loop(0, dests, emit, 0)


def block_rows(chan, own, past):
    head = chan * (own // 2)
    tail = -(-chan * ((past + 1) // 2) // 16) * 16
    return head, tail


def spectra(pieces, place, taps, tables, frames, dests, chan, part=0, parts=1, into=None):
    fine, taps_n = taps.shape[1], taps.shape[0]
    base = fine // RADIX
    keep = chan * dests
    per_res = keep // RADIX
    own, past = PEERS * frames, taps_n - 1
    head_pairs, tail_pairs = own // 2, (past + 1) // 2
    pitch = head_pairs + PITCH
    quads = (head_pairs + tail_pairs + 1) // 2
    step = min(base, 128)
    head_rows, tail_rows = block_rows(chan, own, past)
    dims = (frames, taps_n, base, per_res, dests, chan, head_rows, tail_rows, step)
    weights = (taps.astype(jnp.float32) * (1.0 / 8192.0)).reshape(taps_n, 2, 2, base)
    weights = weights.transpose(2, 3, 1, 0).reshape(2, base, 2 * taps_n)
    blocks = [piece.reshape(frames, 2, base, LANES) for piece in pieces]
    whole = lambda shape: pl.BlockSpec(shape, lambda i, p: (0,) * len(shape))
    return pl.pallas_call(
        functools.partial(spectra_kernel, dims),
        grid_spec=pltpu.PrefetchScalarGridSpec(
            num_scalar_prefetch=1,
            grid=(base // step,),
            in_specs=[pl.BlockSpec((frames, 2, step, LANES), lambda i, p: (0, 0, i, 0))] * PEERS
            + [whole(weights.shape)]
            + [whole(table.shape) for table in tables]
            + [pl.BlockSpec(memory_space=pl.ANY)] * (into is not None),
            out_specs=pl.BlockSpec((dests, head_rows + tail_rows, LANES), lambda i, p: (0, part, 0)),
            scratch_shapes=[
                pltpu.VMEM((own, 2, step, LANES), jnp.float32),
                pltpu.VMEM((2, 2 * (head_pairs + tail_pairs), 16, LANES), jnp.float32),
                pltpu.VMEM((quads, RADIX * base, 2 * LANES), jnp.bfloat16),
                pltpu.VMEM((keep * pitch, LANES), jnp.float32),
                pltpu.VMEM((keep * tail_pairs + 16, LANES), jnp.float32),
            ],
        ),
        out_shape=jax.ShapeDtypeStruct((dests, parts * (head_rows + tail_rows), LANES), jnp.bfloat16),
        input_output_aliases={} if into is None else {PEERS + 4: 0},
        compiler_params=pltpu.CompilerParams(vmem_limit_bytes=56 * MIB),
        name="spectra",
    )(place, *blocks, weights, *tables, *([] if into is None else [into]))


def sort_kernel(dims, source, out, tails):
    planes, cores, own, past, chan = dims
    head_pairs, tail_pairs = own // 2, (past + 1) // 2
    head_rows, tail_rows = block_rows(chan, own, past)
    depth = planes * own
    per_step = out.shape[0]
    at = pl.program_id(0)

    @pl.when(at == 0)
    def _():
        def widen(d, carry):
            tails[d, pl.ds(0, tail_rows), :] = source[d, pl.ds(head_rows, tail_rows), :].astype(jnp.float32)
            tails[d, pl.ds(tail_rows, 8), :] = jnp.zeros((8, LANES), jnp.float32)
            return carry

        lax.fori_loop(0, (planes - 1) * PEERS * cores, widen, 0)

    early = lax.broadcasted_iota(jnp.int32, (head_pairs, LANES), 0) < tail_pairs
    head_at = pl.ds(pl.multiple_of(at * per_step * head_pairs, 16), per_step * head_pairs)
    for z in range(planes):
        for c in range(cores):
            both = [source[(z * PEERS + q) * cores + c, head_at, :].astype(jnp.float32) for q in range(PEERS)]
            for e in range(per_step):
                value = [v[e * head_pairs : (e + 1) * head_pairs] for v in both]
                if z:
                    tail_at = pl.ds((at * per_step + e) * tail_pairs, head_pairs)
                    for q in range(PEERS):
                        late = tails[((z - 1) * PEERS + q) * cores + c, tail_at, :]
                        value[q] = value[q] + jnp.where(early, late, 0.0)
                value = blocks_transposed(value)
                for part in range(2):
                    rows = jnp.concatenate([value[part], value[2 + part]], 0).astype(jnp.bfloat16)
                    out[e, pl.ds(part * depth + z * own, own), pl.ds(c * LANES, LANES)] = rows


def sort(received, part, planes, cores, own, past, chan):
    head_rows, tail_rows = block_rows(chan, own, past)
    per_step = 2
    shape = (chan, 2 * planes * own, cores * LANES)
    return pl.pallas_call(
        functools.partial(sort_kernel, (planes, cores, own, past, chan)),
        grid=(chan // per_step,),
        in_specs=[pl.BlockSpec((received.shape[0], head_rows + tail_rows, LANES), lambda i: (0, part, 0))],
        out_specs=pl.BlockSpec((per_step, *shape[1:]), lambda i: (i, 0, 0)),
        scratch_shapes=[pltpu.VMEM((received.shape[0], tail_rows + 8, LANES), jnp.float32)],
        out_shape=jax.ShapeDtypeStruct(shape, jnp.bfloat16),
        compiler_params=pltpu.CompilerParams(vmem_limit_bytes=40 * MIB),
        name="sort",
    )(received)


def gram_kernel(dims, *refs):
    here, chunks, cores, scale, last = dims
    ins = refs[:here]
    out, stacked, turned, rows_out, cols_out, sems = refs[here + last :]
    per_step = ins[0].shape[0]
    depth = ins[0].shape[1] // 2
    width = here * LANES
    at, steps = pl.program_id(0), pl.num_programs(0)
    slot = at % 2
    exact = math.frexp(scale)[0] == 0.5

    def copies(step):
        half = step % 2
        moves = []
        for e in range(per_step):
            ch = step * per_step + e
            for c in range(cores):
                base = c * chunks * LANES
                if last:
                    old = width - LANES
                    moves.append((rows_out.at[half, e, c], out.at[ch, pl.ds(base + old, LANES), :]))
                    for d in range(cores):
                        moves.append(
                            (
                                cols_out.at[half, e, pl.ds(c * old, old), pl.ds(d * LANES, LANES)],
                                out.at[ch, pl.ds(base, old), pl.ds(d * chunks * LANES + old, LANES)],
                            )
                        )
                else:
                    for d in range(cores):
                        moves.append(
                            (
                                rows_out.at[half, e, pl.ds(c * width, width), pl.ds(d * width, width)],
                                out.at[ch, pl.ds(base, width), pl.ds(d * chunks * LANES, width)],
                            )
                        )
        return [pltpu.make_async_copy(a, b, sems.at[half, k]) for k, (a, b) in enumerate(moves)]

    @pl.when(at >= 2)
    def _():
        for copy in copies(at - 2):
            copy.wait()

    for e in range(per_step):
        for c in range(cores):
            for h in range(here):
                block = ins[h][e, :, c * LANES : (c + 1) * LANES]
                column = pl.ds((c * here + h) * LANES, LANES)
                stacked[e, :, column] = block
                turned[e, 0:depth, column] = -block[depth:]
                turned[e, depth:, column] = block[:depth]

    def left(e, lo, hi):
        value = stacked[e, :, lo:hi].T
        return value * jnp.bfloat16(scale) if exact else value

    def product(rows, value):
        value = jnp.dot(rows, value, preferred_element_type=jnp.float32)
        return value if exact else value * scale

    def narrow(value):
        return value.astype(jnp.bfloat16)

    def diagonal(size):
        shape = (size, size)
        return lax.broadcasted_iota(jnp.int32, shape, 0) <= lax.broadcasted_iota(jnp.int32, shape, 1)

    inputs = cores * width
    if last:
        old = width - LANES
        mask = diagonal(LANES)
        for e in range(per_step):
            for c in range(cores):
                rows = left(e, c * width, c * width + old)
                columns = [
                    (stacked if c <= d else turned)[e, :, d * width + old : (d + 1) * width] for d in range(cores)
                ]
                cols_out[slot, e, pl.ds(c * old, old), :] = narrow(product(rows, jnp.concatenate(columns, 1)))
                lo, hi = c * width + old, (c + 1) * width
                rows = left(e, lo, hi)
                rows_out[slot, e, c, :, 0:lo] = narrow(product(rows, turned[e, :, 0:lo]))
                mixed = jnp.where(mask, product(rows, stacked[e, :, lo:hi]), product(rows, turned[e, :, lo:hi]))
                rows_out[slot, e, c, :, lo:hi] = narrow(mixed)
                if hi < inputs:
                    rows_out[slot, e, c, :, hi:inputs] = narrow(product(rows, stacked[e, :, hi:inputs]))
    else:
        block = 2 * LANES
        mask = diagonal(block)
        for e in range(per_step):
            for i in range(inputs // block):
                lo, hi = i * block, (i + 1) * block
                rows, place = left(e, lo, hi), pl.ds(lo, block)
                if lo:
                    rows_out[slot, e, place, 0:lo] = narrow(product(rows, turned[e, :, 0:lo]))
                mixed = jnp.where(mask, product(rows, stacked[e, :, lo:hi]), product(rows, turned[e, :, lo:hi]))
                rows_out[slot, e, place, lo:hi] = narrow(mixed)
                if hi < inputs:
                    rows_out[slot, e, place, hi:inputs] = narrow(product(rows, stacked[e, :, hi:inputs]))

    for copy in copies(at):
        copy.start()

    @pl.when(at == steps - 1)
    def _():
        if steps > 1:
            for copy in copies(at - 1):
                copy.wait()
        for copy in copies(at):
            copy.wait()


def gram(sorted_chunks, chunks, cores, scale, before=None):
    chan, depth, wide = sorted_chunks[0].shape
    here = len(sorted_chunks)
    last = before is not None
    per_step = 2
    inputs = cores * here * LANES
    old = (here - 1) * LANES
    count = per_step * (cores + cores * cores if last else cores * cores)
    rows_shape = (2, per_step, cores, LANES, inputs) if last else (2, per_step, inputs, inputs)
    cols_shape = (2, per_step, cores * old, cores * LANES) if last else (16, LANES)
    total = cores * chunks * LANES
    return pl.pallas_call(
        functools.partial(gram_kernel, (here, chunks, cores, scale, last)),
        grid=(chan // per_step,),
        in_specs=[pl.BlockSpec((per_step, depth, wide), lambda i: (i, 0, 0))] * here
        + [pl.BlockSpec(memory_space=pl.ANY)] * last,
        out_specs=pl.BlockSpec(memory_space=pl.ANY),
        scratch_shapes=[
            pltpu.VMEM((per_step, depth, inputs), jnp.bfloat16),
            pltpu.VMEM((per_step, depth, inputs), jnp.bfloat16),
            pltpu.VMEM(rows_shape, jnp.bfloat16),
            pltpu.VMEM(cols_shape, jnp.bfloat16),
            pltpu.SemaphoreType.DMA((2, count)),
        ],
        out_shape=jax.ShapeDtypeStruct((chan, total, total), jnp.bfloat16),
        input_output_aliases={here: 0} if last else {},
        compiler_params=pltpu.CompilerParams(vmem_limit_bytes=56 * MIB),
        name="gram_last" if last else "gram_first",
    )(*sorted_chunks, *([before] if last else []))


PITCH = 1
GROUPS = [[0], [1], [2], [3]]
FIRST = False
TIES = [4, 4, 4]


def per_device(voltages, taps):
    past, fine = taps.shape[0] - 1, taps.shape[1]
    frames = voltages.shape[1] // fine
    chunks = voltages.shape[2] // LANES
    n_time, n_group = lax.axis_size("tm"), lax.axis_size("inp")
    dests = n_time * n_group
    chan = KEEP // dests
    own = PEERS * frames
    place = jnp.bitwise_and(lax.axis_index("tm"), PEERS - 1).astype(jnp.int32)[None]
    tables = [jnp.asarray(table.astype(jnp.bfloat16)) for table in dft_tables(fine, KEEP)]

    planes, scale = n_time // PEERS, 1.0 / (n_time * frames)

    def sent(h, after):
        here = lax.optimization_barrier((place, after))[0] if after else place
        pieces = pack(voltages, here, h, fine)
        others = [lax.ppermute(pieces[k], "tm", [(t, t ^ k) for t in range(n_time)]) for k in range(1, PEERS)]
        return [pieces[0], *others]

    groups = GROUPS if chunks == 4 else [[h] for h in range(chunks)]
    moved = [sent(0, [])]
    packed = moved[0][0]
    received, ordered = [], [None] * chunks
    for g, group in enumerate(groups):
        mine = None
        for part, h in enumerate(group):
            if g >= 2 and not part:
                moved[h][0], received[g - 2] = lax.optimization_barrier((moved[h][0], received[g - 2]))
            if h == 0:
                moved.append(sent(1, [packed, moved[0][1]] if FIRST else [packed]))
            mine = spectra(moved[h], place, taps, tables, frames, dests, chan, part, len(group), mine)
            if h == 0 and len(groups[1]) > 1:
                moved.append(sent(2, [moved[1][1]]))
            elif h + 2 < chunks and len(moved) < h + 3:
                moved.append(sent(h + 2, [mine]))
        h += 1
        if h < chunks:
            k = TIES[g]
            mine, moved[h][1:k] = lax.optimization_barrier((mine, moved[h][1:k]))
        if received:
            mine, received[-1] = lax.optimization_barrier((mine, received[-1]))
        received.append(lax.all_to_all(mine, ("tm", "inp"), split_axis=0, concat_axis=0, tiled=True))
    for array, group in zip(received, groups):
        for part, h in enumerate(group):
            ordered[h] = sort(array, part, planes, n_group, own, past, chan)
    first = gram(ordered[:-1], chunks, n_group, scale)
    return gram(ordered, chunks, n_group, scale, first)


def solution(mesh):
    return jax.shard_map(
        per_device,
        mesh=mesh,
        in_specs=(P(None, "tm", "inp"), P()),
        out_specs=P(("tm", "inp"), None, None),
        check_vma=False,
    )
```

```python
import functools
import math

import jax
import jax.numpy as jnp
import numpy as np
from jax import lax
from jax.experimental import pallas as pl
from jax.experimental.pallas import tpu as pltpu
from jax.sharding import PartitionSpec as P

KEEP = 512
RADIX = 4
LANES = 128
PEERS = 4
SUB = LANES // PEERS
MIB = 1 << 20


def dft_tables(fine, keep):
    base = fine // RADIX
    branch = np.arange(base)[None, :]
    channel = np.arange(keep)[:, None]
    phase = np.mod(branch * (channel - keep // 2), fine)
    angle = 2.0 * np.pi / fine * phase
    norm = 1.0 / math.sqrt(fine)
    cosine = (np.cos(angle) * norm).reshape(keep // RADIX, RADIX, base)
    sine = (-np.sin(angle) * norm).reshape(keep // RADIX, RADIX, base)
    plain = np.stack([np.concatenate([cosine[:, c], sine[:, c]]) for c in (0, 2)])
    odd = [
        np.block([[cosine[:, c], sign * sine[:, c]], [sine[:, c], -sign * cosine[:, c]]])
        for c, sign in ((1, 1.0), (3, -1.0))
    ]
    return plain.astype(np.float32), np.concatenate(odd).astype(np.float32)


def lane(shape):
    return lax.broadcasted_iota(jnp.int32, shape, len(shape) - 1)


def blocks_transposed(x):
    low = lane(x[0].shape) < 2 * SUB
    even = lane(x[0].shape) % (2 * SUB) < SUB
    mid = [None] * 4
    for i in range(2):
        a, b = x[i], x[i + 2]
        mid[i] = jnp.where(low, a, pltpu.roll(b, 2 * SUB, 1))
        mid[i + 2] = jnp.where(low, pltpu.roll(a, 2 * SUB, 1), b)
    out = []
    for i in (0, 2):
        a, b = mid[i], mid[i + 1]
        out.append(jnp.where(even, a, pltpu.roll(b, SUB, 1)))
        out.append(jnp.where(even, pltpu.roll(a, LANES - SUB, 1), b))
    return out


def pack_kernel(chunk, place, source, *refs):
    outs, (select, held, sems) = refs[:PEERS], refs[PEERS:]
    frames, rows = held.shape[1], held.shape[3]
    copies = [
        pltpu.make_async_copy(source.at[:, f, :, :, pl.ds(chunk * LANES, LANES)], held.at[:, f], sems.at[f])
        for f in range(frames)
    ]
    for copy in copies:
        copy.start()
    shape = select.shape
    row, column = (lax.broadcasted_iota(jnp.int32, shape, axis) for axis in range(2))
    peer = jnp.bitwise_xor(column // LANES, place[0])
    wanted = (column % LANES) // SUB * LANES + peer * SUB + column % SUB
    select[...] = jnp.where(row == wanted, 1.0, 0.0).astype(jnp.bfloat16)
    for f in range(frames):
        copies[f].wait()
        x = jnp.concatenate([held[r, f, upper] for upper in range(2) for r in range(2)], 1)
        moved = jnp.dot(x, select[...], preferred_element_type=jnp.float32).astype(jnp.bfloat16)
        for k in range(PEERS):
            outs[k][pl.ds(f * rows, rows), :] = moved[:, k * LANES : (k + 1) * LANES]


def pack(voltages, place, chunk, fine):
    frames = voltages.shape[1] // fine
    rows = fine // 2
    shaped = voltages.reshape(2, frames, 2, rows, voltages.shape[2])
    shaped = pltpu.with_memory_space_constraint(shaped, pltpu.HBM)
    return pl.pallas_call(
        functools.partial(pack_kernel, chunk),
        in_specs=[pl.BlockSpec(memory_space=pltpu.SMEM), pl.BlockSpec(memory_space=pltpu.HBM)],
        out_specs=[pl.BlockSpec((frames * rows, LANES), lambda: (0, 0))] * PEERS,
        scratch_shapes=[
            pltpu.VMEM((PEERS * LANES, PEERS * LANES), jnp.bfloat16),
            pltpu.VMEM((2, frames, 2, rows, LANES), jnp.bfloat16),
            pltpu.SemaphoreType.DMA((frames,)),
        ],
        out_shape=[jax.ShapeDtypeStruct((frames * rows, LANES), jnp.bfloat16)] * PEERS,
        compiler_params=pltpu.CompilerParams(vmem_limit_bytes=40 * MIB),
        name="pack",
    )(place, shaped)


def spectra_kernel(dims, place, *refs):
    frames, taps_n, base, per_res, dests, chan, head_rows, tail_rows, step = dims
    pieces = refs[:PEERS]
    taps, plain, odd = refs[PEERS : PEERS + 3]
    out, xs, ys, zs, heads, tails = refs[-6:]
    own = PEERS * frames
    past = taps_n - 1
    total = own + past
    half = LANES // 2
    head_pairs, tail_pairs = own // 2, (past + 1) // 2
    pitch = heads.shape[0] // (per_res * RADIX)
    at = pl.program_id(0)

    for k in range(PEERS):
        first = jnp.bitwise_xor(place[0], k) * frames
        for f in range(frames):
            xs[first + f] = pieces[k][f].astype(jnp.float32)

    low = lane((8, LANES)) < half
    low16 = lane((16, LANES)) < half
    flip = jnp.where(low16, 1.0, -1.0)

    if total % 2:

        @pl.when(at == 0)
        def _():
            ys[:, total] = jnp.zeros(ys.shape[:1] + ys.shape[2:], ys.dtype)

    def filter_rows(b, carry):
        row = pl.multiple_of(b * 16, 16)
        for q in range(2):
            for s in range(2):
                here = pl.ds(pl.multiple_of(row + 8 * s, 8), 8)
                weight = taps[q, pl.ds(pl.multiple_of(at * step + row + 8 * s, 8), 8), :]
                wide = [jnp.broadcast_to(weight[:, k : k + 1], (8, LANES)) for k in range(2 * taps_n)]
                weights = [jnp.where(low, wide[k], wide[k + taps_n]) for k in range(taps_n)]
                x = [xs[f, q, here, :] for f in range(own)]
                for f in range(total):
                    parts = [weights[k] * x[f - k] for k in range(taps_n) if 0 <= f - k < own]
                    while len(parts) > 1:
                        parts = [sum(parts[i : i + 2]) for i in range(0, len(parts), 2)]
                    ys[q, f, pl.ds(8 * s, 8), :] = parts[0]
        for pair in range(head_pairs + tail_pairs):

            def sum_and_difference(q):
                first, second = ys[q, 2 * pair], ys[q, 2 * pair + 1]
                kept = jnp.where(low16, first, second)
                other = pltpu.roll(jnp.where(low16, second, first), half, 1)
                return kept + other, (kept - other) * flip

            a_sum, a_diff = sum_and_difference(0)
            b_sum, b_diff = sum_and_difference(1)
            side = pl.ds((pair % 2) * LANES, LANES)
            for part, value in enumerate((a_sum + b_sum, a_sum - b_sum, a_diff, b_diff)):
                rows = pl.ds(pl.multiple_of(part * base + at * step + row, 16), 16)
                zs[pair // 2, rows, side] = value.astype(jnp.bfloat16)
        return carry

    lax.fori_loop(0, step // 16, filter_rows, 0)

    @pl.when(at == pl.num_programs(0) - 1)
    def _():
        even = lane((per_res, LANES)) % (2 * SUB) < SUB

        def keep(quad, c, both):
            for u in range(2):
                sine = both[per_res:, u * LANES : (u + 1) * LANES]
                turned = jnp.where(even, -pltpu.roll(sine, LANES - SUB, 1), pltpu.roll(sine, SUB, 1))
                value = both[:per_res, u * LANES : (u + 1) * LANES] + turned
                pair = quad * 2 + u
                if pair < head_pairs:
                    heads[pl.ds(c * pitch + pair, per_res, stride=RADIX * pitch), :] = value
                elif pair < head_pairs + tail_pairs:
                    tails[pl.ds(c * tail_pairs + pair - head_pairs, per_res, stride=RADIX * tail_pairs), :] = value

        for quad in range((head_pairs + tail_pairs + 1) // 2):
            for i in range(2):
                rows = zs[quad, i * base : (i + 1) * base]
                keep(quad, 2 * i, jnp.dot(plain[i], rows, preferred_element_type=jnp.float32))
            both = jnp.dot(odd[...], zs[quad, 2 * base :], preferred_element_type=jnp.float32)
            keep(quad, 1, both[: 2 * per_res])
            keep(quad, 3, both[2 * per_res :])

        def emit(d, carry):
            for e in range(0, chan, 16 // head_pairs):
                rows = [heads[pl.ds((d * chan + e + i) * pitch, head_pairs), :] for i in range(16 // head_pairs)]
                out[d, pl.ds(e * head_pairs, 16), :] = jnp.concatenate(rows, 0).astype(jnp.bfloat16)
            out[d, pl.ds(head_rows, tail_rows), :] = tails[
                pl.ds(pl.multiple_of(d * chan * tail_pairs, 8), tail_rows), :
            ].astype(jnp.bfloat16)
            return carry

        lax.fori_loop(0, dests, emit, 0)


def block_rows(chan, own, past):
    head = chan * (own // 2)
    tail = -(-chan * ((past + 1) // 2) // 16) * 16
    return head, tail


def spectra(pieces, place, taps, tables, frames, dests, chan, part=0, parts=1, into=None):
    fine, taps_n = taps.shape[1], taps.shape[0]
    base = fine // RADIX
    keep = chan * dests
    per_res = keep // RADIX
    own, past = PEERS * frames, taps_n - 1
    head_pairs, tail_pairs = own // 2, (past + 1) // 2
    pitch = head_pairs + PITCH
    quads = (head_pairs + tail_pairs + 1) // 2
    step = min(base, 128)
    head_rows, tail_rows = block_rows(chan, own, past)
    dims = (frames, taps_n, base, per_res, dests, chan, head_rows, tail_rows, step)
    weights = (taps.astype(jnp.float32) * (1.0 / 8192.0)).reshape(taps_n, 2, 2, base)
    weights = weights.transpose(2, 3, 1, 0).reshape(2, base, 2 * taps_n)
    blocks = [piece.reshape(frames, 2, base, LANES) for piece in pieces]
    whole = lambda shape: pl.BlockSpec(shape, lambda i, p: (0,) * len(shape))
    return pl.pallas_call(
        functools.partial(spectra_kernel, dims),
        grid_spec=pltpu.PrefetchScalarGridSpec(
            num_scalar_prefetch=1,
            grid=(base // step,),
            in_specs=[pl.BlockSpec((frames, 2, step, LANES), lambda i, p: (0, 0, i, 0))] * PEERS
            + [whole(weights.shape)]
            + [whole(table.shape) for table in tables]
            + [pl.BlockSpec(memory_space=pl.ANY)] * (into is not None),
            out_specs=pl.BlockSpec((dests, head_rows + tail_rows, LANES), lambda i, p: (0, part, 0)),
            scratch_shapes=[
                pltpu.VMEM((own, 2, step, LANES), jnp.float32),
                pltpu.VMEM((2, 2 * (head_pairs + tail_pairs), 16, LANES), jnp.float32),
                pltpu.VMEM((quads, RADIX * base, 2 * LANES), jnp.bfloat16),
                pltpu.VMEM((keep * pitch, LANES), jnp.float32),
                pltpu.VMEM((keep * tail_pairs + 16, LANES), jnp.float32),
            ],
        ),
        out_shape=jax.ShapeDtypeStruct((dests, parts * (head_rows + tail_rows), LANES), jnp.bfloat16),
        input_output_aliases={} if into is None else {PEERS + 4: 0},
        compiler_params=pltpu.CompilerParams(vmem_limit_bytes=56 * MIB),
        name="spectra",
    )(place, *blocks, weights, *tables, *([] if into is None else [into]))


def sort_kernel(dims, source, out, tails):
    planes, cores, own, past, chan = dims
    head_pairs, tail_pairs = own // 2, (past + 1) // 2
    head_rows, tail_rows = block_rows(chan, own, past)
    depth = planes * own
    per_step = out.shape[0]
    at = pl.program_id(0)

    @pl.when(at == 0)
    def _():
        def widen(d, carry):
            tails[d, pl.ds(0, tail_rows), :] = source[d, pl.ds(head_rows, tail_rows), :].astype(jnp.float32)
            tails[d, pl.ds(tail_rows, 8), :] = jnp.zeros((8, LANES), jnp.float32)
            return carry

        lax.fori_loop(0, (planes - 1) * PEERS * cores, widen, 0)

    early = lax.broadcasted_iota(jnp.int32, (head_pairs, LANES), 0) < tail_pairs
    head_at = pl.ds(pl.multiple_of(at * per_step * head_pairs, 16), per_step * head_pairs)
    for z in range(planes):
        for c in range(cores):
            both = [source[(z * PEERS + q) * cores + c, head_at, :].astype(jnp.float32) for q in range(PEERS)]
            for e in range(per_step):
                value = [v[e * head_pairs : (e + 1) * head_pairs] for v in both]
                if z:
                    tail_at = pl.ds((at * per_step + e) * tail_pairs, head_pairs)
                    for q in range(PEERS):
                        late = tails[((z - 1) * PEERS + q) * cores + c, tail_at, :]
                        value[q] = value[q] + jnp.where(early, late, 0.0)
                value = blocks_transposed(value)
                for part in range(2):
                    rows = jnp.concatenate([value[part], value[2 + part]], 0).astype(jnp.bfloat16)
                    out[e, pl.ds(part * depth + z * own, own), pl.ds(c * LANES, LANES)] = rows


def sort(received, part, planes, cores, own, past, chan):
    head_rows, tail_rows = block_rows(chan, own, past)
    per_step = min(chan, SORT_STEP)
    shape = (chan, 2 * planes * own, cores * LANES)
    return pl.pallas_call(
        functools.partial(sort_kernel, (planes, cores, own, past, chan)),
        grid=(chan // per_step,),
        in_specs=[pl.BlockSpec((received.shape[0], head_rows + tail_rows, LANES), lambda i: (0, part, 0))],
        out_specs=pl.BlockSpec((per_step, *shape[1:]), lambda i: (i, 0, 0)),
        scratch_shapes=[pltpu.VMEM((received.shape[0], tail_rows + 8, LANES), jnp.float32)],
        out_shape=jax.ShapeDtypeStruct(shape, jnp.bfloat16),
        compiler_params=pltpu.CompilerParams(vmem_limit_bytes=40 * MIB),
        name="sort",
    )(received)


def gram_kernel(dims, *refs):
    here, chunks, cores, scale, last = dims
    ins = refs[:here]
    out, stacked, turned, rows_out, cols_out, sems = refs[here + last :]
    per_step = ins[0].shape[0]
    depth = ins[0].shape[1] // 2
    width = here * LANES
    at, steps = pl.program_id(0), pl.num_programs(0)
    slot = at % 2
    exact = math.frexp(scale)[0] == 0.5

    def copies(step, channels=None):
        half = step % 2
        moves = []
        for e in range(per_step) if channels is None else channels:
            ch = step * per_step + e
            for c in range(cores):
                base = c * chunks * LANES
                if last:
                    old = width - LANES
                    moves.append((rows_out.at[half, e, c], out.at[ch, pl.ds(base + old, LANES), :]))
                    for d in range(cores):
                        moves.append(
                            (
                                cols_out.at[half, e, pl.ds(c * old, old), pl.ds(d * LANES, LANES)],
                                out.at[ch, pl.ds(base, old), pl.ds(d * chunks * LANES + old, LANES)],
                            )
                        )
                else:
                    for d in range(cores):
                        moves.append(
                            (
                                rows_out.at[half, e, pl.ds(c * width, width), pl.ds(d * width, width)],
                                out.at[ch, pl.ds(base, width), pl.ds(d * chunks * LANES, width)],
                            )
                        )
        skip = 0 if channels is None else channels[0] * len(moves)
        return [pltpu.make_async_copy(a, b, sems.at[half, skip + k]) for k, (a, b) in enumerate(moves)]

    @pl.when(at >= 2)
    def _():
        for copy in copies(at - 2):
            copy.wait()

    for e in range(per_step):
        for c in range(cores):
            for h in range(here):
                block = ins[h][e, :, c * LANES : (c + 1) * LANES]
                column = pl.ds((c * here + h) * LANES, LANES)
                stacked[e, :, column] = block
                turned[e, 0:depth, column] = -block[depth:]
                turned[e, depth:, column] = block[:depth]

    def left(e, lo, hi):
        value = stacked[e, :, lo:hi].T
        return value * jnp.bfloat16(scale) if exact else value

    def product(rows, value):
        value = jnp.dot(rows, value, preferred_element_type=jnp.float32)
        return value if exact else value * scale

    def narrow(value):
        return value.astype(jnp.bfloat16)

    def diagonal(size):
        shape = (size, size)
        return lax.broadcasted_iota(jnp.int32, shape, 0) <= lax.broadcasted_iota(jnp.int32, shape, 1)

    inputs = cores * width
    if last:
        old = width - LANES
        mask = diagonal(LANES)
        for e in range(per_step):
            for c in range(cores):
                rows = left(e, c * width, c * width + old)
                columns = [
                    (stacked if c <= d else turned)[e, :, d * width + old : (d + 1) * width] for d in range(cores)
                ]
                cols_out[slot, e, pl.ds(c * old, old), :] = narrow(product(rows, jnp.concatenate(columns, 1)))
                lo, hi = c * width + old, (c + 1) * width
                rows = left(e, lo, hi)
                rows_out[slot, e, c, :, 0:lo] = narrow(product(rows, turned[e, :, 0:lo]))
                mixed = jnp.where(mask, product(rows, stacked[e, :, lo:hi]), product(rows, turned[e, :, lo:hi]))
                rows_out[slot, e, c, :, lo:hi] = narrow(mixed)
                if hi < inputs:
                    rows_out[slot, e, c, :, hi:inputs] = narrow(product(rows, stacked[e, :, hi:inputs]))
            for copy in copies(at, [e]):
                copy.start()
    else:
        block = 2 * LANES
        mask = diagonal(block)
        for e in range(per_step):
            for i in range(inputs // block):
                lo, hi = i * block, (i + 1) * block
                rows, place = left(e, lo, hi), pl.ds(lo, block)
                if lo:
                    rows_out[slot, e, place, 0:lo] = narrow(product(rows, turned[e, :, 0:lo]))
                mixed = jnp.where(mask, product(rows, stacked[e, :, lo:hi]), product(rows, turned[e, :, lo:hi]))
                rows_out[slot, e, place, lo:hi] = narrow(mixed)
                if hi < inputs:
                    rows_out[slot, e, place, hi:inputs] = narrow(product(rows, stacked[e, :, hi:inputs]))
            for copy in copies(at, [e]):
                copy.start()

    @pl.when(at == steps - 1)
    def _():
        if steps > 1:
            for copy in copies(at - 1):
                copy.wait()
        for copy in copies(at):
            copy.wait()


def gram(sorted_chunks, chunks, cores, scale, before=None):
    chan, depth, wide = sorted_chunks[0].shape
    here = len(sorted_chunks)
    last = before is not None
    per_step = min(chan, PER_STEP)
    inputs = cores * here * LANES
    old = (here - 1) * LANES
    count = per_step * (cores + cores * cores if last else cores * cores)
    rows_shape = (2, per_step, cores, LANES, inputs) if last else (2, per_step, inputs, inputs)
    cols_shape = (2, per_step, cores * old, cores * LANES) if last else (16, LANES)
    total = cores * chunks * LANES
    return pl.pallas_call(
        functools.partial(gram_kernel, (here, chunks, cores, scale, last)),
        grid=(chan // per_step,),
        in_specs=[pl.BlockSpec((per_step, depth, wide), lambda i: (i, 0, 0))] * here
        + [pl.BlockSpec(memory_space=pl.ANY)] * last,
        out_specs=pl.BlockSpec(memory_space=pl.ANY),
        scratch_shapes=[
            pltpu.VMEM((per_step, depth, inputs), jnp.bfloat16),
            pltpu.VMEM((per_step, depth, inputs), jnp.bfloat16),
            pltpu.VMEM(rows_shape, jnp.bfloat16),
            pltpu.VMEM(cols_shape, jnp.bfloat16),
            pltpu.SemaphoreType.DMA((2, count)),
        ],
        out_shape=jax.ShapeDtypeStruct((chan, total, total), jnp.bfloat16),
        input_output_aliases={here: 0} if last else {},
        compiler_params=pltpu.CompilerParams(vmem_limit_bytes=56 * MIB),
        name="gram_last" if last else "gram_first",
    )(*sorted_chunks, *([before] if last else []))


PITCH = 1
PER_STEP = 4
SORT_STEP = 2
FIRST = False
WAIT = True
TIES = [4, 4, 4]


def per_device(voltages, taps):
    past, fine = taps.shape[0] - 1, taps.shape[1]
    frames = voltages.shape[1] // fine
    chunks = voltages.shape[2] // LANES
    n_time, n_group = lax.axis_size("tm"), lax.axis_size("inp")
    dests = n_time * n_group
    chan = KEEP // dests
    own = PEERS * frames
    place = jnp.bitwise_and(lax.axis_index("tm"), PEERS - 1).astype(jnp.int32)[None]
    tables = [jnp.asarray(table.astype(jnp.bfloat16)) for table in dft_tables(fine, KEEP)]

    planes, scale = n_time // PEERS, 1.0 / (n_time * frames)

    def sent(pieces, after):
        if after:
            pieces = lax.optimization_barrier((pieces, after))[0]
        others = [lax.ppermute(pieces[k], "tm", [(t, t ^ k) for t in range(n_time)]) for k in range(1, PEERS)]
        return [pieces[0], *others]

    packed = [pack(voltages, place, 0, fine)]
    later = lax.optimization_barrier((place, packed[0]))[0]
    packed += [pack(voltages, later, h, fine) for h in range(1, chunks)]
    moved = [sent(packed[0], [])]
    moved.append(sent(packed[1], [moved[0][1]] if FIRST else []))
    received = []
    for h in range(chunks):
        if h >= 2:
            moved[h][0], received[h - 2] = lax.optimization_barrier((moved[h][0], received[h - 2]))
        if h == 0:
            moved[0][0], packed = lax.optimization_barrier((moved[0][0], packed))
        mine = spectra(moved[h], place, taps, tables, frames, dests, chan)
        if h + 2 < chunks:
            moved.append(sent(packed[h + 2], [mine] if WAIT else []))
        if h + 1 < chunks:
            k = TIES[h]
            mine, moved[h + 1][1:k] = lax.optimization_barrier((mine, moved[h + 1][1:k]))
        if received:
            mine, received[-1] = lax.optimization_barrier((mine, received[-1]))
        received.append(lax.all_to_all(mine, ("tm", "inp"), split_axis=0, concat_axis=0, tiled=True))
    ordered = [sort(array, 0, planes, n_group, own, past, chan) for array in received]
    first = gram(ordered[:-1], chunks, n_group, scale)
    return gram(ordered, chunks, n_group, scale, first)


def solution(mesh):
    return jax.shard_map(
        per_device,
        mesh=mesh,
        in_specs=(P(None, "tm", "inp"), P()),
        out_specs=P(("tm", "inp"), None, None),
        check_vma=False,
    )
```

```python
import functools
import math

import jax
import jax.numpy as jnp
import numpy as np
from jax import lax
from jax.experimental import pallas as pl
from jax.experimental.pallas import tpu as pltpu
from jax.sharding import PartitionSpec as P

KEEP = 512
RADIX = 4
LANES = 128
PEERS = 4
SUB = LANES // PEERS
MIB = 1 << 20


def dft_tables(fine, keep):
    base = fine // RADIX
    branch = np.arange(base)[None, :]
    channel = np.arange(keep)[:, None]
    phase = np.mod(branch * (channel - keep // 2), fine)
    angle = 2.0 * np.pi / fine * phase
    norm = 1.0 / math.sqrt(fine)
    cosine = (np.cos(angle) * norm).reshape(keep // RADIX, RADIX, base)
    sine = (-np.sin(angle) * norm).reshape(keep // RADIX, RADIX, base)
    plain = np.stack([np.concatenate([cosine[:, c], sine[:, c]]) for c in (0, 2)])
    odd = [
        np.block([[cosine[:, c], sign * sine[:, c]], [sine[:, c], -sign * cosine[:, c]]])
        for c, sign in ((1, 1.0), (3, -1.0))
    ]
    return plain.astype(np.float32), np.concatenate(odd).astype(np.float32)


def lane(shape):
    return lax.broadcasted_iota(jnp.int32, shape, len(shape) - 1)


def blocks_transposed(x):
    low = lane(x[0].shape) < 2 * SUB
    even = lane(x[0].shape) % (2 * SUB) < SUB
    mid = [None] * 4
    for i in range(2):
        a, b = x[i], x[i + 2]
        mid[i] = jnp.where(low, a, pltpu.roll(b, 2 * SUB, 1))
        mid[i + 2] = jnp.where(low, pltpu.roll(a, 2 * SUB, 1), b)
    out = []
    for i in (0, 2):
        a, b = mid[i], mid[i + 1]
        out.append(jnp.where(even, a, pltpu.roll(b, SUB, 1)))
        out.append(jnp.where(even, pltpu.roll(a, LANES - SUB, 1), b))
    return out


def pack_kernel(chunk, place, source, *refs):
    outs, (select, held, sems) = refs[:PEERS], refs[PEERS:]
    frames, rows = held.shape[1], held.shape[3]
    copies = [
        pltpu.make_async_copy(source.at[:, f, :, :, pl.ds(chunk * LANES, LANES)], held.at[:, f], sems.at[f])
        for f in range(frames)
    ]
    for copy in copies:
        copy.start()
    shape = select.shape
    row, column = (lax.broadcasted_iota(jnp.int32, shape, axis) for axis in range(2))
    peer = jnp.bitwise_xor(column // LANES, place[0])
    wanted = (column % LANES) // SUB * LANES + peer * SUB + column % SUB
    select[...] = jnp.where(row == wanted, 1.0, 0.0).astype(jnp.bfloat16)
    for f in range(frames):
        copies[f].wait()
        x = jnp.concatenate([held[r, f, upper] for upper in range(2) for r in range(2)], 1)
        moved = jnp.dot(x, select[...], preferred_element_type=jnp.float32).astype(jnp.bfloat16)
        for k in range(PEERS):
            outs[k][pl.ds(f * rows, rows), :] = moved[:, k * LANES : (k + 1) * LANES]


def pack(voltages, place, chunk, fine):
    frames = voltages.shape[1] // fine
    rows = fine // 2
    shaped = voltages.reshape(2, frames, 2, rows, voltages.shape[2])
    shaped = pltpu.with_memory_space_constraint(shaped, pltpu.HBM)
    return pl.pallas_call(
        functools.partial(pack_kernel, chunk),
        in_specs=[pl.BlockSpec(memory_space=pltpu.SMEM), pl.BlockSpec(memory_space=pltpu.HBM)],
        out_specs=[pl.BlockSpec((frames * rows, LANES), lambda: (0, 0))] * PEERS,
        scratch_shapes=[
            pltpu.VMEM((PEERS * LANES, PEERS * LANES), jnp.bfloat16),
            pltpu.VMEM((2, frames, 2, rows, LANES), jnp.bfloat16),
            pltpu.SemaphoreType.DMA((frames,)),
        ],
        out_shape=[jax.ShapeDtypeStruct((frames * rows, LANES), jnp.bfloat16)] * PEERS,
        compiler_params=pltpu.CompilerParams(vmem_limit_bytes=40 * MIB),
        name="pack",
    )(place, shaped)


def spectra_kernel(dims, place, *refs):
    frames, taps_n, base, per_res, dests, chan, head_rows, tail_rows, step = dims
    pieces = refs[:PEERS]
    taps, plain, odd = refs[PEERS : PEERS + 3]
    out, xs, ys, zs, heads, tails = refs[-6:]
    own = PEERS * frames
    past = taps_n - 1
    total = own + past
    half = LANES // 2
    head_pairs, tail_pairs = own // 2, (past + 1) // 2
    pitch = heads.shape[0] // (per_res * RADIX)
    at = pl.program_id(0)

    for k in range(PEERS):
        first = jnp.bitwise_xor(place[0], k) * frames
        for f in range(frames):
            xs[first + f] = pieces[k][f].astype(jnp.float32)

    low = lane((8, LANES)) < half
    low16 = lane((16, LANES)) < half
    flip = jnp.where(low16, 1.0, -1.0)

    if total % 2:

        @pl.when(at == 0)
        def _():
            ys[:, total] = jnp.zeros(ys.shape[:1] + ys.shape[2:], ys.dtype)

    def filter_rows(b, carry):
        row = pl.multiple_of(b * 16, 16)
        for q in range(2):
            for s in range(2):
                here = pl.ds(pl.multiple_of(row + 8 * s, 8), 8)
                weight = taps[q, pl.ds(pl.multiple_of(at * step + row + 8 * s, 8), 8), :]
                wide = [jnp.broadcast_to(weight[:, k : k + 1], (8, LANES)) for k in range(2 * taps_n)]
                weights = [jnp.where(low, wide[k], wide[k + taps_n]) for k in range(taps_n)]
                x = [xs[f, q, here, :] for f in range(own)]
                for f in range(total):
                    parts = [weights[k] * x[f - k] for k in range(taps_n) if 0 <= f - k < own]
                    while len(parts) > 1:
                        parts = [sum(parts[i : i + 2]) for i in range(0, len(parts), 2)]
                    ys[q, f, pl.ds(8 * s, 8), :] = parts[0]
        for pair in range(head_pairs + tail_pairs):

            def sum_and_difference(q):
                first, second = ys[q, 2 * pair], ys[q, 2 * pair + 1]
                kept = jnp.where(low16, first, second)
                other = pltpu.roll(jnp.where(low16, second, first), half, 1)
                return kept + other, (kept - other) * flip

            a_sum, a_diff = sum_and_difference(0)
            b_sum, b_diff = sum_and_difference(1)
            side = pl.ds((pair % 2) * LANES, LANES)
            for part, value in enumerate((a_sum + b_sum, a_sum - b_sum, a_diff, b_diff)):
                rows = pl.ds(pl.multiple_of(part * base + at * step + row, 16), 16)
                zs[pair // 2, rows, side] = value.astype(jnp.bfloat16)
        return carry

    lax.fori_loop(0, step // 16, filter_rows, 0)

    @pl.when(at == pl.num_programs(0) - 1)
    def _():
        even = lane((per_res, LANES)) % (2 * SUB) < SUB

        def keep(quad, c, both):
            for u in range(2):
                sine = both[per_res:, u * LANES : (u + 1) * LANES]
                turned = jnp.where(even, -pltpu.roll(sine, LANES - SUB, 1), pltpu.roll(sine, SUB, 1))
                value = both[:per_res, u * LANES : (u + 1) * LANES] + turned
                pair = quad * 2 + u
                if pair < head_pairs:
                    heads[pl.ds(c * pitch + pair, per_res, stride=RADIX * pitch), :] = value
                elif pair < head_pairs + tail_pairs:
                    tails[pl.ds(c * tail_pairs + pair - head_pairs, per_res, stride=RADIX * tail_pairs), :] = value

        for quad in range((head_pairs + tail_pairs + 1) // 2):
            for i in range(2):
                rows = zs[quad, i * base : (i + 1) * base]
                keep(quad, 2 * i, jnp.dot(plain[i], rows, preferred_element_type=jnp.float32))
            both = jnp.dot(odd[...], zs[quad, 2 * base :], preferred_element_type=jnp.float32)
            keep(quad, 1, both[: 2 * per_res])
            keep(quad, 3, both[2 * per_res :])

        def emit(d, carry):
            for e in range(0, chan, 16 // head_pairs):
                rows = [heads[pl.ds((d * chan + e + i) * pitch, head_pairs), :] for i in range(16 // head_pairs)]
                out[d, pl.ds(e * head_pairs, 16), :] = jnp.concatenate(rows, 0).astype(jnp.bfloat16)
            out[d, pl.ds(head_rows, tail_rows), :] = tails[
                pl.ds(pl.multiple_of(d * chan * tail_pairs, 8), tail_rows), :
            ].astype(jnp.bfloat16)
            return carry

        lax.fori_loop(0, dests, emit, 0)


def block_rows(chan, own, past):
    head = chan * (own // 2)
    tail = -(-chan * ((past + 1) // 2) // 16) * 16
    return head, tail


def spectra(pieces, place, taps, tables, frames, dests, chan, part=0, parts=1, into=None):
    fine, taps_n = taps.shape[1], taps.shape[0]
    base = fine // RADIX
    keep = chan * dests
    per_res = keep // RADIX
    own, past = PEERS * frames, taps_n - 1
    head_pairs, tail_pairs = own // 2, (past + 1) // 2
    pitch = head_pairs + PITCH
    quads = (head_pairs + tail_pairs + 1) // 2
    step = min(base, 128)
    head_rows, tail_rows = block_rows(chan, own, past)
    dims = (frames, taps_n, base, per_res, dests, chan, head_rows, tail_rows, step)
    weights = (taps.astype(jnp.float32) * (1.0 / 8192.0)).reshape(taps_n, 2, 2, base)
    weights = weights.transpose(2, 3, 1, 0).reshape(2, base, 2 * taps_n)
    blocks = [piece.reshape(frames, 2, base, LANES) for piece in pieces]
    whole = lambda shape: pl.BlockSpec(shape, lambda i, p: (0,) * len(shape))
    return pl.pallas_call(
        functools.partial(spectra_kernel, dims),
        grid_spec=pltpu.PrefetchScalarGridSpec(
            num_scalar_prefetch=1,
            grid=(base // step,),
            in_specs=[pl.BlockSpec((frames, 2, step, LANES), lambda i, p: (0, 0, i, 0))] * PEERS
            + [whole(weights.shape)]
            + [whole(table.shape) for table in tables]
            + [pl.BlockSpec(memory_space=pl.ANY)] * (into is not None),
            out_specs=pl.BlockSpec((dests, head_rows + tail_rows, LANES), lambda i, p: (0, part, 0)),
            scratch_shapes=[
                pltpu.VMEM((own, 2, step, LANES), jnp.float32),
                pltpu.VMEM((2, 2 * (head_pairs + tail_pairs), 16, LANES), jnp.float32),
                pltpu.VMEM((quads, RADIX * base, 2 * LANES), jnp.bfloat16),
                pltpu.VMEM((keep * pitch, LANES), jnp.float32),
                pltpu.VMEM((keep * tail_pairs + 16, LANES), jnp.float32),
            ],
        ),
        out_shape=jax.ShapeDtypeStruct((dests, parts * (head_rows + tail_rows), LANES), jnp.bfloat16),
        input_output_aliases={} if into is None else {PEERS + 4: 0},
        compiler_params=pltpu.CompilerParams(vmem_limit_bytes=56 * MIB),
        name="spectra",
    )(place, *blocks, weights, *tables, *([] if into is None else [into]))


def in_order(dims, source, tails, at, per_step, store):
    planes, cores, own, past, chan = dims
    head_pairs, tail_pairs = own // 2, (past + 1) // 2
    head_rows, tail_rows = block_rows(chan, own, past)
    depth = planes * own

    @pl.when(at == 0)
    def _():
        def widen(d, carry):
            tails[d, pl.ds(0, tail_rows), :] = source[d, pl.ds(head_rows, tail_rows), :].astype(jnp.float32)
            tails[d, pl.ds(tail_rows, 8), :] = jnp.zeros((8, LANES), jnp.float32)
            return carry

        lax.fori_loop(0, (planes - 1) * PEERS * cores, widen, 0)

    early = lax.broadcasted_iota(jnp.int32, (head_pairs, LANES), 0) < tail_pairs
    head_at = pl.ds(pl.multiple_of(at * per_step * head_pairs, 16), per_step * head_pairs)
    for z in range(planes):
        for c in range(cores):
            both = [source[(z * PEERS + q) * cores + c, head_at, :].astype(jnp.float32) for q in range(PEERS)]
            for e in range(per_step):
                value = [v[e * head_pairs : (e + 1) * head_pairs] for v in both]
                if z:
                    tail_at = pl.ds((at * per_step + e) * tail_pairs, head_pairs)
                    for q in range(PEERS):
                        late = tails[((z - 1) * PEERS + q) * cores + c, tail_at, :]
                        value[q] = value[q] + jnp.where(early, late, 0.0)
                value = blocks_transposed(value)
                for part in range(2):
                    rows = jnp.concatenate([value[part], value[2 + part]], 0).astype(jnp.bfloat16)
                    store(e, pl.ds(part * depth + z * own, own), c, rows)


def sort_kernel(dims, source, out, tails):
    def store(e, rows, c, value):
        out[e, rows, pl.ds(c * LANES, LANES)] = value

    in_order(dims, source, tails, pl.program_id(0), out.shape[0], store)


def sort(received, part, planes, cores, own, past, chan):
    head_rows, tail_rows = block_rows(chan, own, past)
    per_step = min(chan, SORT_STEP)
    shape = (chan, 2 * planes * own, cores * LANES)
    return pl.pallas_call(
        functools.partial(sort_kernel, (planes, cores, own, past, chan)),
        grid=(chan // per_step,),
        in_specs=[pl.BlockSpec((received.shape[0], head_rows + tail_rows, LANES), lambda i: (0, part, 0))],
        out_specs=pl.BlockSpec((per_step, *shape[1:]), lambda i: (i, 0, 0)),
        scratch_shapes=[pltpu.VMEM((received.shape[0], tail_rows + 8, LANES), jnp.float32)],
        out_shape=jax.ShapeDtypeStruct(shape, jnp.bfloat16),
        compiler_params=pltpu.CompilerParams(vmem_limit_bytes=40 * MIB),
        name="sort",
    )(received)


def gram_kernel(dims, *refs):
    here, chunks, cores, scale, last = dims[:5]
    ins = refs[: here - last]
    out, stacked, turned, rows_out, cols_out, sems = refs[here + last : here + last + 6]
    per_step = ins[0].shape[0]
    depth = ins[0].shape[1] // 2
    width = here * LANES
    at, steps = pl.program_id(0), pl.num_programs(0)
    slot = at % 2
    exact = math.frexp(scale)[0] == 0.5

    def copies(step, channels=None):
        half = step % 2
        moves = []
        for e in range(per_step) if channels is None else channels:
            ch = step * per_step + e
            for c in range(cores):
                base = c * chunks * LANES
                if last:
                    old = width - LANES
                    moves.append((rows_out.at[half, e, c], out.at[ch, pl.ds(base + old, LANES), :]))
                    for d in range(cores):
                        moves.append(
                            (
                                cols_out.at[half, e, pl.ds(c * old, old), pl.ds(d * LANES, LANES)],
                                out.at[ch, pl.ds(base, old), pl.ds(d * chunks * LANES + old, LANES)],
                            )
                        )
                else:
                    for d in range(cores):
                        moves.append(
                            (
                                rows_out.at[half, e, pl.ds(c * width, width), pl.ds(d * width, width)],
                                out.at[ch, pl.ds(base, width), pl.ds(d * chunks * LANES, width)],
                            )
                        )
        skip = 0 if channels is None else channels[0] * len(moves)
        return [pltpu.make_async_copy(a, b, sems.at[half, skip + k]) for k, (a, b) in enumerate(moves)]

    @pl.when(at >= 2)
    def _():
        for copy in copies(at - 2):
            copy.wait()

    if last:

        def store(e, rows, c, value):
            stacked[e, rows, pl.ds((c * here + here - 1) * LANES, LANES)] = value

        in_order(dims[5], refs[here - 1], refs[-1], at, per_step, store)

    for e in range(per_step):
        for c in range(cores):
            for h in range(here):
                column = pl.ds((c * here + h) * LANES, LANES)
                if h < len(ins):
                    block = ins[h][e, :, c * LANES : (c + 1) * LANES]
                    stacked[e, :, column] = block
                else:
                    block = stacked[e, :, column]
                turned[e, 0:depth, column] = -block[depth:]
                turned[e, depth:, column] = block[:depth]

    def left(e, lo, hi):
        value = stacked[e, :, lo:hi].T
        return value * jnp.bfloat16(scale) if exact else value

    def product(rows, value):
        value = jnp.dot(rows, value, preferred_element_type=jnp.float32)
        return value if exact else value * scale

    def narrow(value):
        return value.astype(jnp.bfloat16)

    def diagonal(size):
        shape = (size, size)
        return lax.broadcasted_iota(jnp.int32, shape, 0) <= lax.broadcasted_iota(jnp.int32, shape, 1)

    inputs = cores * width
    if last:
        old = width - LANES
        mask = diagonal(LANES)
        for e in range(per_step):
            for c in range(cores):
                rows = left(e, c * width, c * width + old)
                columns = [
                    (stacked if c <= d else turned)[e, :, d * width + old : (d + 1) * width] for d in range(cores)
                ]
                cols_out[slot, e, pl.ds(c * old, old), :] = narrow(product(rows, jnp.concatenate(columns, 1)))
                lo, hi = c * width + old, (c + 1) * width
                rows = left(e, lo, hi)
                rows_out[slot, e, c, :, 0:lo] = narrow(product(rows, turned[e, :, 0:lo]))
                mixed = jnp.where(mask, product(rows, stacked[e, :, lo:hi]), product(rows, turned[e, :, lo:hi]))
                rows_out[slot, e, c, :, lo:hi] = narrow(mixed)
                if hi < inputs:
                    rows_out[slot, e, c, :, hi:inputs] = narrow(product(rows, stacked[e, :, hi:inputs]))
            for copy in copies(at, [e]):
                copy.start()
    else:
        block = 2 * LANES
        mask = diagonal(block)
        for e in range(per_step):
            for i in range(inputs // block):
                lo, hi = i * block, (i + 1) * block
                rows, place = left(e, lo, hi), pl.ds(lo, block)
                if lo:
                    rows_out[slot, e, place, 0:lo] = narrow(product(rows, turned[e, :, 0:lo]))
                mixed = jnp.where(mask, product(rows, stacked[e, :, lo:hi]), product(rows, turned[e, :, lo:hi]))
                rows_out[slot, e, place, lo:hi] = narrow(mixed)
                if hi < inputs:
                    rows_out[slot, e, place, hi:inputs] = narrow(product(rows, stacked[e, :, hi:inputs]))
            for copy in copies(at, [e]):
                copy.start()

    @pl.when(at == steps - 1)
    def _():
        if steps > 1:
            for copy in copies(at - 1):
                copy.wait()
        for copy in copies(at):
            copy.wait()


def gram(sorted_chunks, chunks, cores, scale, before=None, fresh=None, order=None):
    chan, depth, wide = sorted_chunks[0].shape
    last = before is not None
    here = len(sorted_chunks) + last
    per_step = min(chan, PER_STEP)
    inputs = cores * here * LANES
    old = (here - 1) * LANES
    count = per_step * (cores + cores * cores if last else cores * cores)
    rows_shape = (2, per_step, cores, LANES, inputs) if last else (2, per_step, inputs, inputs)
    cols_shape = (2, per_step, cores * old, cores * LANES) if last else (16, LANES)
    total = cores * chunks * LANES
    return pl.pallas_call(
        functools.partial(gram_kernel, (here, chunks, cores, scale, last, order)),
        grid=(chan // per_step,),
        in_specs=[pl.BlockSpec((per_step, depth, wide), lambda i: (i, 0, 0))] * (here - last)
        + ([pl.BlockSpec(fresh.shape, lambda i: (0, 0, 0))] if last else [])
        + [pl.BlockSpec(memory_space=pl.ANY)] * last,
        out_specs=pl.BlockSpec(memory_space=pl.ANY),
        scratch_shapes=[
            pltpu.VMEM((per_step, depth, inputs), jnp.bfloat16),
            pltpu.VMEM((per_step, depth, inputs), jnp.bfloat16),
            pltpu.VMEM(rows_shape, jnp.bfloat16),
            pltpu.VMEM(cols_shape, jnp.bfloat16),
            pltpu.SemaphoreType.DMA((2, count)),
        ]
        + ([pltpu.VMEM((fresh.shape[0], block_rows(chan, *order[2:4])[1] + 8, LANES), jnp.float32)] if last else []),
        out_shape=jax.ShapeDtypeStruct((chan, total, total), jnp.bfloat16),
        input_output_aliases={here: 0} if last else {},
        compiler_params=pltpu.CompilerParams(vmem_limit_bytes=56 * MIB),
        name="gram_last" if last else "gram_first",
    )(*sorted_chunks, *([fresh, before] if last else []))


PITCH = 1
PER_STEP = 4
SORT_STEP = 2
FIRST = False
WAIT = True
TIES = [4, 4, 4]


def per_device(voltages, taps):
    past, fine = taps.shape[0] - 1, taps.shape[1]
    frames = voltages.shape[1] // fine
    chunks = voltages.shape[2] // LANES
    n_time, n_group = lax.axis_size("tm"), lax.axis_size("inp")
    dests = n_time * n_group
    chan = KEEP // dests
    own = PEERS * frames
    place = jnp.bitwise_and(lax.axis_index("tm"), PEERS - 1).astype(jnp.int32)[None]
    tables = [jnp.asarray(table.astype(jnp.bfloat16)) for table in dft_tables(fine, KEEP)]

    planes, scale = n_time // PEERS, 1.0 / (n_time * frames)

    def sent(pieces, after):
        if after:
            pieces = lax.optimization_barrier((pieces, after))[0]
        others = [lax.ppermute(pieces[k], "tm", [(t, t ^ k) for t in range(n_time)]) for k in range(1, PEERS)]
        return [pieces[0], *others]

    packed = [pack(voltages, place, 0, fine)]
    later = lax.optimization_barrier((place, packed[0]))[0]
    packed += [pack(voltages, later, h, fine) for h in range(1, chunks)]
    moved = [sent(packed[0], [])]
    moved.append(sent(packed[1], [moved[0][1]] if FIRST else []))
    received = []
    for h in range(chunks):
        if h >= 2:
            moved[h][0], received[h - 2] = lax.optimization_barrier((moved[h][0], received[h - 2]))
        if h == 0:
            moved[0][0], packed = lax.optimization_barrier((moved[0][0], packed))
        mine = spectra(moved[h], place, taps, tables, frames, dests, chan)
        if h + 2 < chunks:
            moved.append(sent(packed[h + 2], [mine] if WAIT else []))
        if h + 1 < chunks:
            k = TIES[h]
            mine, moved[h + 1][1:k] = lax.optimization_barrier((mine, moved[h + 1][1:k]))
        if received:
            mine, received[-1] = lax.optimization_barrier((mine, received[-1]))
        received.append(lax.all_to_all(mine, ("tm", "inp"), split_axis=0, concat_axis=0, tiled=True))
    ordered = [sort(array, 0, planes, n_group, own, past, chan) for array in received[:-1]]
    first = gram(ordered, chunks, n_group, scale)
    return gram(ordered, chunks, n_group, scale, first, received[-1], (planes, n_group, own, past, chan))


def solution(mesh):
    return jax.shard_map(
        per_device,
        mesh=mesh,
        in_specs=(P(None, "tm", "inp"), P()),
        out_specs=P(("tm", "inp"), None, None),
        check_vma=False,
    )
```

```python
import functools
import math

import jax
import jax.numpy as jnp
import numpy as np
from jax import lax
from jax.experimental import pallas as pl
from jax.experimental.pallas import tpu as pltpu
from jax.sharding import PartitionSpec as P

KEEP = 512
RADIX = 4
LANES = 128
PEERS = 4
SUB = LANES // PEERS
MIB = 1 << 20
PITCH = 1
PER_STEP = 4
SORT_STEP = 2


def dft_tables(fine, keep):
    base = fine // RADIX
    branch = np.arange(base)[None, :]
    channel = np.arange(keep)[:, None]
    phase = np.mod(branch * (channel - keep // 2), fine)
    angle = 2.0 * np.pi / fine * phase
    norm = 1.0 / math.sqrt(fine)
    cosine = (np.cos(angle) * norm).reshape(keep // RADIX, RADIX, base)
    sine = (-np.sin(angle) * norm).reshape(keep // RADIX, RADIX, base)
    plain = np.stack([np.concatenate([cosine[:, c], sine[:, c]]) for c in (0, 2)])
    odd = [
        np.block([[cosine[:, c], sign * sine[:, c]], [sine[:, c], -sign * cosine[:, c]]])
        for c, sign in ((1, 1.0), (3, -1.0))
    ]
    return plain.astype(np.float32), np.concatenate(odd).astype(np.float32)


def lane(shape):
    return lax.broadcasted_iota(jnp.int32, shape, len(shape) - 1)


def blocks_transposed(x):
    low = lane(x[0].shape) < 2 * SUB
    even = lane(x[0].shape) % (2 * SUB) < SUB
    mid = [None] * 4
    for i in range(2):
        a, b = x[i], x[i + 2]
        mid[i] = jnp.where(low, a, pltpu.roll(b, 2 * SUB, 1))
        mid[i + 2] = jnp.where(low, pltpu.roll(a, 2 * SUB, 1), b)
    out = []
    for i in (0, 2):
        a, b = mid[i], mid[i + 1]
        out.append(jnp.where(even, a, pltpu.roll(b, SUB, 1)))
        out.append(jnp.where(even, pltpu.roll(a, LANES - SUB, 1), b))
    return out


def pack_kernel(chunk, place, source, *refs):
    outs, (select, held, sems) = refs[:PEERS], refs[PEERS:]
    frames, rows = held.shape[1], held.shape[3]
    copies = [
        pltpu.make_async_copy(source.at[:, f, :, :, pl.ds(chunk * LANES, LANES)], held.at[:, f], sems.at[f])
        for f in range(frames)
    ]
    for copy in copies:
        copy.start()
    shape = select.shape
    row, column = (lax.broadcasted_iota(jnp.int32, shape, axis) for axis in range(2))
    peer = jnp.bitwise_xor(column // LANES, place[0])
    wanted = (column % LANES) // SUB * LANES + peer * SUB + column % SUB
    select[...] = jnp.where(row == wanted, 1.0, 0.0).astype(jnp.bfloat16)
    for f in range(frames):
        copies[f].wait()
        x = jnp.concatenate([held[r, f, upper] for upper in range(2) for r in range(2)], 1)
        moved = jnp.dot(x, select[...], preferred_element_type=jnp.float32).astype(jnp.bfloat16)
        for k in range(PEERS):
            outs[k][pl.ds(f * rows, rows), :] = moved[:, k * LANES : (k + 1) * LANES]


def pack(voltages, place, chunk, fine):
    frames = voltages.shape[1] // fine
    rows = fine // 2
    shaped = voltages.reshape(2, frames, 2, rows, voltages.shape[2])
    shaped = pltpu.with_memory_space_constraint(shaped, pltpu.HBM)
    return pl.pallas_call(
        functools.partial(pack_kernel, chunk),
        in_specs=[pl.BlockSpec(memory_space=pltpu.SMEM), pl.BlockSpec(memory_space=pltpu.HBM)],
        out_specs=[pl.BlockSpec((frames * rows, LANES), lambda: (0, 0))] * PEERS,
        scratch_shapes=[
            pltpu.VMEM((PEERS * LANES, PEERS * LANES), jnp.bfloat16),
            pltpu.VMEM((2, frames, 2, rows, LANES), jnp.bfloat16),
            pltpu.SemaphoreType.DMA((frames,)),
        ],
        out_shape=[jax.ShapeDtypeStruct((frames * rows, LANES), jnp.bfloat16)] * PEERS,
        compiler_params=pltpu.CompilerParams(vmem_limit_bytes=40 * MIB),
        name="pack",
    )(place, shaped)


def spectra_kernel(dims, place, *refs):
    frames, taps_n, base, per_res, dests, chan, head_rows, tail_rows, step = dims
    pieces = refs[:PEERS]
    taps, plain, odd = refs[PEERS : PEERS + 3]
    out, xs, ys, zs, heads, tails = refs[-6:]
    own = PEERS * frames
    past = taps_n - 1
    total = own + past
    half = LANES // 2
    head_pairs, tail_pairs = own // 2, (past + 1) // 2
    pitch = heads.shape[0] // (per_res * RADIX)
    at = pl.program_id(0)

    for k in range(PEERS):
        first = jnp.bitwise_xor(place[0], k) * frames
        for f in range(frames):
            xs[first + f] = pieces[k][f].astype(jnp.float32)

    low = lane((8, LANES)) < half
    low16 = lane((16, LANES)) < half
    flip = jnp.where(low16, 1.0, -1.0)

    if total % 2:

        @pl.when(at == 0)
        def _():
            ys[:, total] = jnp.zeros(ys.shape[:1] + ys.shape[2:], ys.dtype)

    def filter_rows(b, carry):
        row = pl.multiple_of(b * 16, 16)
        for q in range(2):
            for s in range(2):
                here = pl.ds(pl.multiple_of(row + 8 * s, 8), 8)
                weight = taps[q, pl.ds(pl.multiple_of(at * step + row + 8 * s, 8), 8), :]
                wide = [jnp.broadcast_to(weight[:, k : k + 1], (8, LANES)) for k in range(2 * taps_n)]
                weights = [jnp.where(low, wide[k], wide[k + taps_n]) for k in range(taps_n)]
                x = [xs[f, q, here, :] for f in range(own)]
                for f in range(total):
                    parts = [weights[k] * x[f - k] for k in range(taps_n) if 0 <= f - k < own]
                    while len(parts) > 1:
                        parts = [sum(parts[i : i + 2]) for i in range(0, len(parts), 2)]
                    ys[q, f, pl.ds(8 * s, 8), :] = parts[0]
        for pair in range(head_pairs + tail_pairs):

            def sum_and_difference(q):
                first, second = ys[q, 2 * pair], ys[q, 2 * pair + 1]
                kept = jnp.where(low16, first, second)
                other = pltpu.roll(jnp.where(low16, second, first), half, 1)
                return kept + other, (kept - other) * flip

            a_sum, a_diff = sum_and_difference(0)
            b_sum, b_diff = sum_and_difference(1)
            side = pl.ds((pair % 2) * LANES, LANES)
            for part, value in enumerate((a_sum + b_sum, a_sum - b_sum, a_diff, b_diff)):
                rows = pl.ds(pl.multiple_of(part * base + at * step + row, 16), 16)
                zs[pair // 2, rows, side] = value.astype(jnp.bfloat16)
        return carry

    lax.fori_loop(0, step // 16, filter_rows, 0)

    @pl.when(at == pl.num_programs(0) - 1)
    def _():
        even = lane((per_res, LANES)) % (2 * SUB) < SUB

        def keep(quad, c, both):
            for u in range(2):
                sine = both[per_res:, u * LANES : (u + 1) * LANES]
                turned = jnp.where(even, -pltpu.roll(sine, LANES - SUB, 1), pltpu.roll(sine, SUB, 1))
                value = both[:per_res, u * LANES : (u + 1) * LANES] + turned
                pair = quad * 2 + u
                if pair < head_pairs:
                    heads[pl.ds(c * pitch + pair, per_res, stride=RADIX * pitch), :] = value
                elif pair < head_pairs + tail_pairs:
                    tails[pl.ds(c * tail_pairs + pair - head_pairs, per_res, stride=RADIX * tail_pairs), :] = value

        for quad in range((head_pairs + tail_pairs + 1) // 2):
            for i in range(2):
                rows = zs[quad, i * base : (i + 1) * base]
                keep(quad, 2 * i, jnp.dot(plain[i], rows, preferred_element_type=jnp.float32))
            both = jnp.dot(odd[...], zs[quad, 2 * base :], preferred_element_type=jnp.float32)
            keep(quad, 1, both[: 2 * per_res])
            keep(quad, 3, both[2 * per_res :])

        def emit(d, carry):
            for e in range(0, chan, 16 // head_pairs):
                rows = [heads[pl.ds((d * chan + e + i) * pitch, head_pairs), :] for i in range(16 // head_pairs)]
                out[d, pl.ds(e * head_pairs, 16), :] = jnp.concatenate(rows, 0).astype(jnp.bfloat16)
            out[d, pl.ds(head_rows, tail_rows), :] = tails[
                pl.ds(pl.multiple_of(d * chan * tail_pairs, 8), tail_rows), :
            ].astype(jnp.bfloat16)
            return carry

        lax.fori_loop(0, dests, emit, 0)


def block_rows(chan, own, past):
    head = chan * (own // 2)
    tail = -(-chan * ((past + 1) // 2) // 16) * 16
    return head, tail


def spectra(pieces, place, taps, tables, frames, dests, chan, part=0, parts=1, into=None):
    fine, taps_n = taps.shape[1], taps.shape[0]
    base = fine // RADIX
    keep = chan * dests
    per_res = keep // RADIX
    own, past = PEERS * frames, taps_n - 1
    head_pairs, tail_pairs = own // 2, (past + 1) // 2
    pitch = head_pairs + PITCH
    quads = (head_pairs + tail_pairs + 1) // 2
    step = min(base, 128)
    head_rows, tail_rows = block_rows(chan, own, past)
    dims = (frames, taps_n, base, per_res, dests, chan, head_rows, tail_rows, step)
    weights = (taps.astype(jnp.float32) * (1.0 / 8192.0)).reshape(taps_n, 2, 2, base)
    weights = weights.transpose(2, 3, 1, 0).reshape(2, base, 2 * taps_n)
    blocks = [piece.reshape(frames, 2, base, LANES) for piece in pieces]
    whole = lambda shape: pl.BlockSpec(shape, lambda i, p: (0,) * len(shape))
    return pl.pallas_call(
        functools.partial(spectra_kernel, dims),
        grid_spec=pltpu.PrefetchScalarGridSpec(
            num_scalar_prefetch=1,
            grid=(base // step,),
            in_specs=[pl.BlockSpec((frames, 2, step, LANES), lambda i, p: (0, 0, i, 0))] * PEERS
            + [whole(weights.shape)]
            + [whole(table.shape) for table in tables]
            + [pl.BlockSpec(memory_space=pl.ANY)] * (into is not None),
            out_specs=pl.BlockSpec((dests, head_rows + tail_rows, LANES), lambda i, p: (0, part, 0)),
            scratch_shapes=[
                pltpu.VMEM((own, 2, step, LANES), jnp.float32),
                pltpu.VMEM((2, 2 * (head_pairs + tail_pairs), 16, LANES), jnp.float32),
                pltpu.VMEM((quads, RADIX * base, 2 * LANES), jnp.bfloat16),
                pltpu.VMEM((keep * pitch + 64, LANES), jnp.float32),
                pltpu.VMEM((keep * tail_pairs + 64, LANES), jnp.float32),
            ],
        ),
        out_shape=jax.ShapeDtypeStruct((dests, parts * (head_rows + tail_rows), LANES), jnp.bfloat16),
        input_output_aliases={} if into is None else {PEERS + 4: 0},
        compiler_params=pltpu.CompilerParams(vmem_limit_bytes=56 * MIB),
        name="spectra",
    )(place, *blocks, weights, *tables, *([] if into is None else [into]))


def in_order(dims, source, tails, at, per_step, store):
    planes, cores, own, past, chan = dims
    head_pairs, tail_pairs = own // 2, (past + 1) // 2
    head_rows, tail_rows = block_rows(chan, own, past)
    depth = planes * own

    @pl.when(at == 0)
    def _():
        def widen(d, carry):
            tails[d, pl.ds(0, tail_rows), :] = source[d, pl.ds(head_rows, tail_rows), :].astype(jnp.float32)
            tails[d, pl.ds(tail_rows, 8), :] = jnp.zeros((8, LANES), jnp.float32)
            return carry

        lax.fori_loop(0, (planes - 1) * PEERS * cores, widen, 0)

    early = lax.broadcasted_iota(jnp.int32, (head_pairs, LANES), 0) < tail_pairs
    head_at = pl.ds(pl.multiple_of(at * per_step * head_pairs, 16), per_step * head_pairs)
    for z in range(planes):
        for c in range(cores):
            both = [source[(z * PEERS + q) * cores + c, head_at, :].astype(jnp.float32) for q in range(PEERS)]
            for e in range(per_step):
                value = [v[e * head_pairs : (e + 1) * head_pairs] for v in both]
                if z:
                    tail_at = pl.ds((at * per_step + e) * tail_pairs, head_pairs)
                    for q in range(PEERS):
                        late = tails[((z - 1) * PEERS + q) * cores + c, tail_at, :]
                        value[q] = value[q] + jnp.where(early, late, 0.0)
                value = blocks_transposed(value)
                for part in range(2):
                    rows = jnp.concatenate([value[part], value[2 + part]], 0).astype(jnp.bfloat16)
                    store(e, pl.ds(part * depth + z * own, own), c, rows)


def sort_kernel(dims, source, out, tails):
    def store(e, rows, c, value):
        out[e, rows, pl.ds(c * LANES, LANES)] = value

    in_order(dims, source, tails, pl.program_id(0), out.shape[0], store)


def sort(received, part, planes, cores, own, past, chan):
    head_rows, tail_rows = block_rows(chan, own, past)
    per_step = min(chan, SORT_STEP)
    shape = (chan, 2 * planes * own, cores * LANES)
    return pl.pallas_call(
        functools.partial(sort_kernel, (planes, cores, own, past, chan)),
        grid=(chan // per_step,),
        in_specs=[pl.BlockSpec((received.shape[0], head_rows + tail_rows, LANES), lambda i: (0, part, 0))],
        out_specs=pl.BlockSpec((per_step, *shape[1:]), lambda i: (i, 0, 0)),
        scratch_shapes=[pltpu.VMEM((received.shape[0], tail_rows + 8, LANES), jnp.float32)],
        out_shape=jax.ShapeDtypeStruct(shape, jnp.bfloat16),
        compiler_params=pltpu.CompilerParams(vmem_limit_bytes=40 * MIB),
        name="sort",
    )(received)


def gram_kernel(dims, *refs):
    here, chunks, cores, scale, last = dims[:5]
    ins = refs[: here - last]
    out, stacked, turned, rows_out, cols_out, sems = refs[here + last : here + last + 6]
    per_step = ins[0].shape[0]
    depth = ins[0].shape[1] // 2
    width = here * LANES
    at, steps = pl.program_id(0), pl.num_programs(0)
    slot = at % 2
    exact = math.frexp(scale)[0] == 0.5

    def copies(step, channels=None):
        half = step % 2
        moves = []
        for e in range(per_step) if channels is None else channels:
            ch = step * per_step + e
            for c in range(cores):
                base = c * chunks * LANES
                if last:
                    old = width - LANES
                    moves.append((rows_out.at[half, e, c], out.at[ch, pl.ds(base + old, LANES), :]))
                    for d in range(cores):
                        moves.append(
                            (
                                cols_out.at[half, e, pl.ds(c * old, old), pl.ds(d * LANES, LANES)],
                                out.at[ch, pl.ds(base, old), pl.ds(d * chunks * LANES + old, LANES)],
                            )
                        )
                else:
                    for d in range(cores):
                        moves.append(
                            (
                                rows_out.at[half, e, pl.ds(c * width, width), pl.ds(d * width, width)],
                                out.at[ch, pl.ds(base, width), pl.ds(d * chunks * LANES, width)],
                            )
                        )
        skip = 0 if channels is None else channels[0] * len(moves)
        return [pltpu.make_async_copy(a, b, sems.at[half, skip + k]) for k, (a, b) in enumerate(moves)]

    @pl.when(at >= 2)
    def _():
        for copy in copies(at - 2):
            copy.wait()

    if last:

        def store(e, rows, c, value):
            stacked[e, rows, pl.ds((c * here + here - 1) * LANES, LANES)] = value

        in_order(dims[5], refs[here - 1], refs[-1], at, per_step, store)

    for e in range(per_step):
        for c in range(cores):
            for h in range(here):
                column = pl.ds((c * here + h) * LANES, LANES)
                if h < len(ins):
                    block = ins[h][e, :, c * LANES : (c + 1) * LANES]
                    stacked[e, :, column] = block
                else:
                    block = stacked[e, :, column]
                turned[e, 0:depth, column] = -block[depth:]
                turned[e, depth:, column] = block[:depth]

    def left(e, lo, hi):
        value = stacked[e, :, lo:hi].T
        return value * jnp.bfloat16(scale) if exact else value

    def product(rows, value):
        value = jnp.dot(rows, value, preferred_element_type=jnp.float32)
        return value if exact else value * scale

    def narrow(value):
        return value.astype(jnp.bfloat16)

    def diagonal(size):
        shape = (size, size)
        return lax.broadcasted_iota(jnp.int32, shape, 0) <= lax.broadcasted_iota(jnp.int32, shape, 1)

    inputs = cores * width
    if last:
        old = width - LANES
        mask = diagonal(LANES)
        for e in range(per_step):
            for c in range(cores):
                rows = left(e, c * width, c * width + old)
                columns = [
                    (stacked if c <= d else turned)[e, :, d * width + old : (d + 1) * width] for d in range(cores)
                ]
                cols_out[slot, e, pl.ds(c * old, old), :] = narrow(product(rows, jnp.concatenate(columns, 1)))
                lo, hi = c * width + old, (c + 1) * width
                rows = left(e, lo, hi)
                rows_out[slot, e, c, :, 0:lo] = narrow(product(rows, turned[e, :, 0:lo]))
                mixed = jnp.where(mask, product(rows, stacked[e, :, lo:hi]), product(rows, turned[e, :, lo:hi]))
                rows_out[slot, e, c, :, lo:hi] = narrow(mixed)
                if hi < inputs:
                    rows_out[slot, e, c, :, hi:inputs] = narrow(product(rows, stacked[e, :, hi:inputs]))
            for copy in copies(at, [e]):
                copy.start()
    else:
        block = 2 * LANES
        mask = diagonal(block)
        for e in range(per_step):
            for i in range(inputs // block):
                lo, hi = i * block, (i + 1) * block
                rows, place = left(e, lo, hi), pl.ds(lo, block)
                if lo:
                    rows_out[slot, e, place, 0:lo] = narrow(product(rows, turned[e, :, 0:lo]))
                mixed = jnp.where(mask, product(rows, stacked[e, :, lo:hi]), product(rows, turned[e, :, lo:hi]))
                rows_out[slot, e, place, lo:hi] = narrow(mixed)
                if hi < inputs:
                    rows_out[slot, e, place, hi:inputs] = narrow(product(rows, stacked[e, :, hi:inputs]))
            for copy in copies(at, [e]):
                copy.start()

    @pl.when(at == steps - 1)
    def _():
        if steps > 1:
            for copy in copies(at - 1):
                copy.wait()
        for copy in copies(at):
            copy.wait()


def gram(sorted_chunks, chunks, cores, scale, before=None, fresh=None, order=None):
    chan, depth, wide = sorted_chunks[0].shape
    last = before is not None
    here = len(sorted_chunks) + last
    per_step = min(chan, PER_STEP)
    inputs = cores * here * LANES
    old = (here - 1) * LANES
    count = per_step * (cores + cores * cores if last else cores * cores)
    rows_shape = (2, per_step, cores, LANES, inputs) if last else (2, per_step, inputs, inputs)
    cols_shape = (2, per_step, cores * old, cores * LANES) if last else (16, LANES)
    total = cores * chunks * LANES
    return pl.pallas_call(
        functools.partial(gram_kernel, (here, chunks, cores, scale, last, order)),
        grid=(chan // per_step,),
        in_specs=[pl.BlockSpec((per_step, depth, wide), lambda i: (i, 0, 0))] * (here - last)
        + ([pl.BlockSpec(fresh.shape, lambda i: (0, 0, 0))] if last else [])
        + [pl.BlockSpec(memory_space=pl.ANY)] * last,
        out_specs=pl.BlockSpec(memory_space=pl.ANY),
        scratch_shapes=[
            pltpu.VMEM((per_step, depth, inputs), jnp.bfloat16),
            pltpu.VMEM((per_step, depth, inputs), jnp.bfloat16),
            pltpu.VMEM(rows_shape, jnp.bfloat16),
            pltpu.VMEM(cols_shape, jnp.bfloat16),
            pltpu.SemaphoreType.DMA((2, count)),
        ]
        + ([pltpu.VMEM((fresh.shape[0], block_rows(chan, *order[2:4])[1] + 8, LANES), jnp.float32)] if last else []),
        out_shape=jax.ShapeDtypeStruct((chan, total, total), jnp.bfloat16),
        input_output_aliases={here: 0} if last else {},
        compiler_params=pltpu.CompilerParams(vmem_limit_bytes=56 * MIB),
        name="gram_last" if last else "gram_first",
    )(*sorted_chunks, *([fresh, before] if last else []))


def per_device(voltages, taps):
    past, fine = taps.shape[0] - 1, taps.shape[1]
    frames = voltages.shape[1] // fine
    chunks = voltages.shape[2] // LANES
    n_time, n_group = lax.axis_size("tm"), lax.axis_size("inp")
    dests = n_time * n_group
    chan = KEEP // dests
    own = PEERS * frames
    place = jnp.bitwise_and(lax.axis_index("tm"), PEERS - 1).astype(jnp.int32)[None]
    tables = [jnp.asarray(table.astype(jnp.bfloat16)) for table in dft_tables(fine, KEEP)]

    planes, scale = n_time // PEERS, 1.0 / (n_time * frames)

    def sent(pieces, after):
        if after:
            pieces = lax.optimization_barrier((pieces, after))[0]
        others = [lax.ppermute(pieces[k], "tm", [(t, t ^ k) for t in range(n_time)]) for k in range(1, PEERS)]
        return [pieces[0], *others]

    packed = [pack(voltages, place, 0, fine)]
    later = lax.optimization_barrier((place, packed[0]))[0]
    packed += [pack(voltages, later, h, fine) for h in range(1, chunks)]
    moved = [sent(packed[0], [])]
    moved.append(sent(packed[1], []))
    received = []
    for h in range(chunks):
        if h >= 2:
            moved[h][0], received[h - 2] = lax.optimization_barrier((moved[h][0], received[h - 2]))
        if h == 0:
            moved[0][0], packed = lax.optimization_barrier((moved[0][0], packed))
        mine = spectra(moved[h], place, taps, tables, frames, dests, chan)
        if h + 2 < chunks:
            moved.append(sent(packed[h + 2], [mine]))
        if h + 1 < chunks:
            mine, moved[h + 1][1:] = lax.optimization_barrier((mine, moved[h + 1][1:]))
        if received:
            mine, received[-1] = lax.optimization_barrier((mine, received[-1]))
        received.append(lax.all_to_all(mine, ("tm", "inp"), split_axis=0, concat_axis=0, tiled=True))
    ordered = [sort(array, 0, planes, n_group, own, past, chan) for array in received[:-1]]
    first = gram(ordered, chunks, n_group, scale)
    return gram(ordered, chunks, n_group, scale, first, received[-1], (planes, n_group, own, past, chan))


def solution(mesh):
    return jax.shard_map(
        per_device,
        mesh=mesh,
        in_specs=(P(None, "tm", "inp"), P()),
        out_specs=P(("tm", "inp"), None, None),
        check_vma=False,
    )
```

```python
import functools
import math

import jax
import jax.numpy as jnp
import numpy as np
from jax import lax
from jax.experimental import pallas as pl
from jax.experimental.pallas import tpu as pltpu
from jax.sharding import PartitionSpec as P

KEEP = 512
RADIX = 4
LANES = 128
PEERS = 4
SUB = LANES // PEERS
MIB = 1 << 20
PITCH = 1
PER_STEP = 4
SORT_STEP = 2


def dft_tables(fine, keep):
    base = fine // RADIX
    branch = np.arange(base)[None, :]
    channel = np.arange(keep)[:, None]
    phase = np.mod(branch * (channel - keep // 2), fine)
    angle = 2.0 * np.pi / fine * phase
    norm = 1.0 / math.sqrt(fine)
    cosine = (np.cos(angle) * norm).reshape(keep // RADIX, RADIX, base)
    sine = (-np.sin(angle) * norm).reshape(keep // RADIX, RADIX, base)
    plain = np.stack([np.concatenate([cosine[:, c], sine[:, c]]) for c in (0, 2)])
    odd = [
        np.block([[cosine[:, c], sign * sine[:, c]], [sine[:, c], -sign * cosine[:, c]]])
        for c, sign in ((1, 1.0), (3, -1.0))
    ]
    return plain.astype(np.float32), np.concatenate(odd).astype(np.float32)


def lane(shape):
    return lax.broadcasted_iota(jnp.int32, shape, len(shape) - 1)


def blocks_transposed(x):
    low = lane(x[0].shape) < 2 * SUB
    even = lane(x[0].shape) % (2 * SUB) < SUB
    mid = [None] * 4
    for i in range(2):
        a, b = x[i], x[i + 2]
        mid[i] = jnp.where(low, a, pltpu.roll(b, 2 * SUB, 1))
        mid[i + 2] = jnp.where(low, pltpu.roll(a, 2 * SUB, 1), b)
    out = []
    for i in (0, 2):
        a, b = mid[i], mid[i + 1]
        out.append(jnp.where(even, a, pltpu.roll(b, SUB, 1)))
        out.append(jnp.where(even, pltpu.roll(a, LANES - SUB, 1), b))
    return out


def pack_kernel(chunk, place, source, *refs):
    outs, (select, held, sems) = refs[:PEERS], refs[PEERS:]
    frames, rows = held.shape[1], held.shape[3]
    copies = [
        pltpu.make_async_copy(source.at[:, f, :, :, pl.ds(chunk * LANES, LANES)], held.at[:, f], sems.at[f])
        for f in range(frames)
    ]
    for copy in copies:
        copy.start()
    shape = select.shape
    row, column = (lax.broadcasted_iota(jnp.int32, shape, axis) for axis in range(2))
    peer = jnp.bitwise_xor(column // LANES, place[0])
    wanted = (column % LANES) // SUB * LANES + peer * SUB + column % SUB
    select[...] = jnp.where(row == wanted, 1.0, 0.0).astype(jnp.bfloat16)
    for f in range(frames):
        copies[f].wait()
        x = jnp.concatenate([held[r, f, upper] for upper in range(2) for r in range(2)], 1)
        moved = jnp.dot(x, select[...], preferred_element_type=jnp.float32).astype(jnp.bfloat16)
        for k in range(PEERS):
            outs[k][pl.ds(f * rows, rows), :] = moved[:, k * LANES : (k + 1) * LANES]


def pack(voltages, place, chunk, fine):
    frames = voltages.shape[1] // fine
    rows = fine // 2
    shaped = voltages.reshape(2, frames, 2, rows, voltages.shape[2])
    shaped = pltpu.with_memory_space_constraint(shaped, pltpu.HBM)
    return pl.pallas_call(
        functools.partial(pack_kernel, chunk),
        in_specs=[pl.BlockSpec(memory_space=pltpu.SMEM), pl.BlockSpec(memory_space=pltpu.HBM)],
        out_specs=[pl.BlockSpec((frames * rows, LANES), lambda: (0, 0))] * PEERS,
        scratch_shapes=[
            pltpu.VMEM((PEERS * LANES, PEERS * LANES), jnp.bfloat16),
            pltpu.VMEM((2, frames, 2, rows, LANES), jnp.bfloat16),
            pltpu.SemaphoreType.DMA((frames,)),
        ],
        out_shape=[jax.ShapeDtypeStruct((frames * rows, LANES), jnp.bfloat16)] * PEERS,
        compiler_params=pltpu.CompilerParams(vmem_limit_bytes=40 * MIB),
        name="pack",
    )(place, shaped)


def spectra_kernel(dims, place, *refs):
    frames, taps_n, base, per_res, dests, chan, head_rows, tail_rows, step = dims
    pieces = refs[:PEERS]
    taps, plain, odd = refs[PEERS : PEERS + 3]
    out, xs, ys, zs, heads, tails = refs[-6:]
    own = PEERS * frames
    past = taps_n - 1
    total = own + past
    half = LANES // 2
    head_pairs, tail_pairs = own // 2, (past + 1) // 2
    pitch = heads.shape[0] // (per_res * RADIX)
    at = pl.program_id(0)

    for k in range(PEERS):
        first = jnp.bitwise_xor(place[0], k) * frames
        for f in range(frames):
            xs[first + f] = pieces[k][f].astype(jnp.float32)

    low = lane((8, LANES)) < half
    low16 = lane((16, LANES)) < half
    flip = jnp.where(low16, 1.0, -1.0)

    if total % 2:

        @pl.when(at == 0)
        def _():
            ys[:, total] = jnp.zeros(ys.shape[:1] + ys.shape[2:], ys.dtype)

    def filter_rows(b, carry):
        row = pl.multiple_of(b * 16, 16)
        for q in range(2):
            for s in range(2):
                here = pl.ds(pl.multiple_of(row + 8 * s, 8), 8)
                weight = taps[q, pl.ds(pl.multiple_of(at * step + row + 8 * s, 8), 8), :]
                wide = [jnp.broadcast_to(weight[:, k : k + 1], (8, LANES)) for k in range(2 * taps_n)]
                weights = [jnp.where(low, wide[k], wide[k + taps_n]) for k in range(taps_n)]
                x = [xs[f, q, here, :] for f in range(own)]
                for f in range(total):
                    parts = [weights[k] * x[f - k] for k in range(taps_n) if 0 <= f - k < own]
                    while len(parts) > 1:
                        parts = [sum(parts[i : i + 2]) for i in range(0, len(parts), 2)]
                    ys[q, f, pl.ds(8 * s, 8), :] = parts[0]
        for pair in range(head_pairs + tail_pairs):

            def sum_and_difference(q):
                first, second = ys[q, 2 * pair], ys[q, 2 * pair + 1]
                kept = jnp.where(low16, first, second)
                other = pltpu.roll(jnp.where(low16, second, first), half, 1)
                return kept + other, (kept - other) * flip

            a_sum, a_diff = sum_and_difference(0)
            b_sum, b_diff = sum_and_difference(1)
            side = pl.ds((pair % 2) * LANES, LANES)
            for part, value in enumerate((a_sum + b_sum, a_sum - b_sum, a_diff, b_diff)):
                rows = pl.ds(pl.multiple_of(part * base + at * step + row, 16), 16)
                zs[pair // 2, rows, side] = value.astype(jnp.bfloat16)
        return carry

    lax.fori_loop(0, step // 16, filter_rows, 0)

    @pl.when(at == pl.num_programs(0) - 1)
    def _():
        even = lane((per_res, LANES)) % (2 * SUB) < SUB

        def keep(quad, c, both):
            for u in range(2):
                sine = both[per_res:, u * LANES : (u + 1) * LANES]
                turned = jnp.where(even, -pltpu.roll(sine, LANES - SUB, 1), pltpu.roll(sine, SUB, 1))
                value = both[:per_res, u * LANES : (u + 1) * LANES] + turned
                pair = quad * 2 + u
                if pair < head_pairs:
                    heads[pl.ds(c * pitch + pair, per_res, stride=RADIX * pitch), :] = value
                elif pair < head_pairs + tail_pairs:
                    tails[pl.ds(c * tail_pairs + pair - head_pairs, per_res, stride=RADIX * tail_pairs), :] = value

        for quad in range((head_pairs + tail_pairs + 1) // 2):
            for i in range(2):
                rows = zs[quad, i * base : (i + 1) * base]
                keep(quad, 2 * i, jnp.dot(plain[i], rows, preferred_element_type=jnp.float32))
            both = jnp.dot(odd[...], zs[quad, 2 * base :], preferred_element_type=jnp.float32)
            keep(quad, 1, both[: 2 * per_res])
            keep(quad, 3, both[2 * per_res :])

        def emit(d, carry):
            for e in range(0, chan, 16 // head_pairs):
                rows = [heads[pl.ds((d * chan + e + i) * pitch, head_pairs), :] for i in range(16 // head_pairs)]
                out[d, pl.ds(e * head_pairs, 16), :] = jnp.concatenate(rows, 0).astype(jnp.bfloat16)
            out[d, pl.ds(head_rows, tail_rows), :] = tails[
                pl.ds(pl.multiple_of(d * chan * tail_pairs, 8), tail_rows), :
            ].astype(jnp.bfloat16)
            return carry

        lax.fori_loop(0, dests, emit, 0)


def block_rows(chan, own, past):
    head = chan * (own // 2)
    tail = -(-chan * ((past + 1) // 2) // 16) * 16
    return head, tail


def spectra(pieces, place, taps, tables, frames, dests, chan, part=0, parts=1, into=None):
    fine, taps_n = taps.shape[1], taps.shape[0]
    base = fine // RADIX
    keep = chan * dests
    per_res = keep // RADIX
    own, past = PEERS * frames, taps_n - 1
    head_pairs, tail_pairs = own // 2, (past + 1) // 2
    pitch = head_pairs + PITCH
    quads = (head_pairs + tail_pairs + 1) // 2
    step = min(base, 128)
    head_rows, tail_rows = block_rows(chan, own, past)
    dims = (frames, taps_n, base, per_res, dests, chan, head_rows, tail_rows, step)
    weights = (taps.astype(jnp.float32) * (1.0 / 8192.0)).reshape(taps_n, 2, 2, base)
    weights = weights.transpose(2, 3, 1, 0).reshape(2, base, 2 * taps_n)
    blocks = [piece.reshape(frames, 2, base, LANES) for piece in pieces]
    whole = lambda shape: pl.BlockSpec(shape, lambda i, p: (0,) * len(shape))
    return pl.pallas_call(
        functools.partial(spectra_kernel, dims),
        grid_spec=pltpu.PrefetchScalarGridSpec(
            num_scalar_prefetch=1,
            grid=(base // step,),
            in_specs=[pl.BlockSpec((frames, 2, step, LANES), lambda i, p: (0, 0, i, 0))] * PEERS
            + [whole(weights.shape)]
            + [whole(table.shape) for table in tables]
            + [pl.BlockSpec(memory_space=pl.ANY)] * (into is not None),
            out_specs=pl.BlockSpec((dests, head_rows + tail_rows, LANES), lambda i, p: (0, part, 0)),
            scratch_shapes=[
                pltpu.VMEM((own, 2, step, LANES), jnp.float32),
                pltpu.VMEM((2, 2 * (head_pairs + tail_pairs), 16, LANES), jnp.float32),
                pltpu.VMEM((quads, RADIX * base, 2 * LANES), jnp.bfloat16),
                pltpu.VMEM((keep * pitch + 64, LANES), jnp.float32),
                pltpu.VMEM((keep * tail_pairs + 64, LANES), jnp.float32),
            ],
        ),
        out_shape=jax.ShapeDtypeStruct((dests, parts * (head_rows + tail_rows), LANES), jnp.bfloat16),
        input_output_aliases={} if into is None else {PEERS + 4: 0},
        compiler_params=pltpu.CompilerParams(vmem_limit_bytes=56 * MIB),
        name="spectra",
    )(place, *blocks, weights, *tables, *([] if into is None else [into]))


def in_order(dims, source, tails, at, per_step, store):
    planes, cores, own, past, chan = dims
    head_pairs, tail_pairs = own // 2, (past + 1) // 2
    head_rows, tail_rows = block_rows(chan, own, past)
    depth = planes * own

    @pl.when(at == 0)
    def _():
        def widen(d, carry):
            tails[d, pl.ds(0, tail_rows), :] = source[d, pl.ds(head_rows, tail_rows), :].astype(jnp.float32)
            tails[d, pl.ds(tail_rows, 8), :] = jnp.zeros((8, LANES), jnp.float32)
            return carry

        lax.fori_loop(0, (planes - 1) * PEERS * cores, widen, 0)

    early = lax.broadcasted_iota(jnp.int32, (head_pairs, LANES), 0) < tail_pairs
    head_at = pl.ds(pl.multiple_of(at * per_step * head_pairs, 16), per_step * head_pairs)
    for z in range(planes):
        for c in range(cores):
            both = [source[(z * PEERS + q) * cores + c, head_at, :].astype(jnp.float32) for q in range(PEERS)]
            for e in range(per_step):
                value = [v[e * head_pairs : (e + 1) * head_pairs] for v in both]
                if z:
                    tail_at = pl.ds((at * per_step + e) * tail_pairs, head_pairs)
                    for q in range(PEERS):
                        late = tails[((z - 1) * PEERS + q) * cores + c, tail_at, :]
                        value[q] = value[q] + jnp.where(early, late, 0.0)
                value = blocks_transposed(value)
                for part in range(2):
                    rows = jnp.concatenate([value[part], value[2 + part]], 0).astype(jnp.bfloat16)
                    store(e, pl.ds(part * depth + z * own, own), c, rows)


def sort_kernel(dims, source, out, tails):
    def store(e, rows, c, value):
        out[e, rows, pl.ds(c * LANES, LANES)] = value

    in_order(dims, source, tails, pl.program_id(0), out.shape[0], store)


def sort(received, part, planes, cores, own, past, chan):
    head_rows, tail_rows = block_rows(chan, own, past)
    per_step = min(chan, SORT_STEP)
    shape = (chan, 2 * planes * own, cores * LANES)
    return pl.pallas_call(
        functools.partial(sort_kernel, (planes, cores, own, past, chan)),
        grid=(chan // per_step,),
        in_specs=[pl.BlockSpec((received.shape[0], head_rows + tail_rows, LANES), lambda i: (0, part, 0))],
        out_specs=pl.BlockSpec((per_step, *shape[1:]), lambda i: (i, 0, 0)),
        scratch_shapes=[pltpu.VMEM((received.shape[0], tail_rows + 8, LANES), jnp.float32)],
        out_shape=jax.ShapeDtypeStruct(shape, jnp.bfloat16),
        compiler_params=pltpu.CompilerParams(vmem_limit_bytes=40 * MIB),
        name="sort",
    )(received)


def gram_kernel(dims, *refs):
    here, chunks, cores, scale, last = dims[:5]
    ins = refs[: here - last]
    out, stacked, turned, rows_out, cols_out, sems = refs[here + last : here + last + 6]
    per_step = ins[0].shape[0]
    depth = ins[0].shape[1] // 2
    width = here * LANES
    at, steps = pl.program_id(0), pl.num_programs(0)
    slot = at % 2

    def copies(step, channels=None):
        half = step % 2
        moves = []
        for e in range(per_step) if channels is None else channels:
            ch = step * per_step + e
            for c in range(cores):
                base = c * chunks * LANES
                if last:
                    old = width - LANES
                    moves.append((rows_out.at[half, e, c], out.at[ch, pl.ds(base + old, LANES), :]))
                    for d in range(cores):
                        moves.append(
                            (
                                cols_out.at[half, e, pl.ds(c * old, old), pl.ds(d * LANES, LANES)],
                                out.at[ch, pl.ds(base, old), pl.ds(d * chunks * LANES + old, LANES)],
                            )
                        )
                else:
                    for d in range(cores):
                        moves.append(
                            (
                                rows_out.at[half, e, pl.ds(c * width, width), pl.ds(d * width, width)],
                                out.at[ch, pl.ds(base, width), pl.ds(d * chunks * LANES, width)],
                            )
                        )
        skip = 0 if channels is None else channels[0] * len(moves)
        return [pltpu.make_async_copy(a, b, sems.at[half, skip + k]) for k, (a, b) in enumerate(moves)]

    @pl.when(at >= 2)
    def _():
        for copy in copies(at - 2):
            copy.wait()

    if last:

        def store(e, rows, c, value):
            stacked[e, rows, pl.ds((c * here + here - 1) * LANES, LANES)] = value

        in_order(dims[5], refs[here - 1], refs[-1], at, per_step, store)

    for e in range(per_step):
        for c in range(cores):
            for h in range(here):
                column = pl.ds((c * here + h) * LANES, LANES)
                if h < len(ins):
                    block = ins[h][e, :, c * LANES : (c + 1) * LANES]
                    stacked[e, :, column] = block
                else:
                    block = stacked[e, :, column]
                turned[e, 0:depth, column] = -block[depth:]
                turned[e, depth:, column] = block[:depth]

    def left(e, lo, hi):
        value = stacked[e, :, lo:hi].T
        return value

    def product(rows, value):
        value = jnp.dot(rows, value, preferred_element_type=jnp.float32)
        return value if scale == 1.0 else value * scale

    def narrow(value):
        return value.astype(jnp.bfloat16)

    def diagonal(size):
        shape = (size, size)
        return lax.broadcasted_iota(jnp.int32, shape, 0) <= lax.broadcasted_iota(jnp.int32, shape, 1)

    inputs = cores * width
    if last:
        old = width - LANES
        mask = diagonal(LANES)
        for e in range(per_step):
            for c in range(cores):
                rows = left(e, c * width, c * width + old)
                columns = [
                    (stacked if c <= d else turned)[e, :, d * width + old : (d + 1) * width] for d in range(cores)
                ]
                cols_out[slot, e, pl.ds(c * old, old), :] = narrow(product(rows, jnp.concatenate(columns, 1)))
                lo, hi = c * width + old, (c + 1) * width
                rows = left(e, lo, hi)
                rows_out[slot, e, c, :, 0:lo] = narrow(product(rows, turned[e, :, 0:lo]))
                mixed = jnp.where(mask, product(rows, stacked[e, :, lo:hi]), product(rows, turned[e, :, lo:hi]))
                rows_out[slot, e, c, :, lo:hi] = narrow(mixed)
                if hi < inputs:
                    rows_out[slot, e, c, :, hi:inputs] = narrow(product(rows, stacked[e, :, hi:inputs]))
            for copy in copies(at, [e]):
                copy.start()
    else:
        block = 2 * LANES
        mask = diagonal(block)
        for e in range(per_step):
            for i in range(inputs // block):
                lo, hi = i * block, (i + 1) * block
                rows, place = left(e, lo, hi), pl.ds(lo, block)
                if lo:
                    rows_out[slot, e, place, 0:lo] = narrow(product(rows, turned[e, :, 0:lo]))
                mixed = jnp.where(mask, product(rows, stacked[e, :, lo:hi]), product(rows, turned[e, :, lo:hi]))
                rows_out[slot, e, place, lo:hi] = narrow(mixed)
                if hi < inputs:
                    rows_out[slot, e, place, hi:inputs] = narrow(product(rows, stacked[e, :, hi:inputs]))
            for copy in copies(at, [e]):
                copy.start()

    @pl.when(at == steps - 1)
    def _():
        if steps > 1:
            for copy in copies(at - 1):
                copy.wait()
        for copy in copies(at):
            copy.wait()


def gram(sorted_chunks, chunks, cores, scale, before=None, fresh=None, order=None):
    chan, depth, wide = sorted_chunks[0].shape
    last = before is not None
    here = len(sorted_chunks) + last
    per_step = min(chan, PER_STEP)
    inputs = cores * here * LANES
    old = (here - 1) * LANES
    count = per_step * (cores + cores * cores if last else cores * cores)
    rows_shape = (2, per_step, cores, LANES, inputs) if last else (2, per_step, inputs, inputs)
    cols_shape = (2, per_step, cores * old, cores * LANES) if last else (16, LANES)
    total = cores * chunks * LANES
    return pl.pallas_call(
        functools.partial(gram_kernel, (here, chunks, cores, scale, last, order)),
        grid=(chan // per_step,),
        in_specs=[pl.BlockSpec((per_step, depth, wide), lambda i: (i, 0, 0))] * (here - last)
        + ([pl.BlockSpec(fresh.shape, lambda i: (0, 0, 0))] if last else [])
        + [pl.BlockSpec(memory_space=pl.ANY)] * last,
        out_specs=pl.BlockSpec(memory_space=pl.ANY),
        scratch_shapes=[
            pltpu.VMEM((per_step, depth, inputs), jnp.bfloat16),
            pltpu.VMEM((per_step, depth, inputs), jnp.bfloat16),
            pltpu.VMEM(rows_shape, jnp.bfloat16),
            pltpu.VMEM(cols_shape, jnp.bfloat16),
            pltpu.SemaphoreType.DMA((2, count)),
        ]
        + ([pltpu.VMEM((fresh.shape[0], block_rows(chan, *order[2:4])[1] + 8, LANES), jnp.float32)] if last else []),
        out_shape=jax.ShapeDtypeStruct((chan, total, total), jnp.bfloat16),
        input_output_aliases={here: 0} if last else {},
        compiler_params=pltpu.CompilerParams(vmem_limit_bytes=56 * MIB),
        name="gram_last" if last else "gram_first",
    )(*sorted_chunks, *([fresh, before] if last else []))


def per_device(voltages, taps):
    past, fine = taps.shape[0] - 1, taps.shape[1]
    frames = voltages.shape[1] // fine
    chunks = voltages.shape[2] // LANES
    n_time, n_group = lax.axis_size("tm"), lax.axis_size("inp")
    dests = n_time * n_group
    chan = KEEP // dests
    own = PEERS * frames
    place = jnp.bitwise_and(lax.axis_index("tm"), PEERS - 1).astype(jnp.int32)[None]
    planes, scale = n_time // PEERS, 1.0 / (n_time * frames)
    root = math.sqrt(scale)
    if math.frexp(root)[0] != 0.5:
        root = 1.0
    scale /= root * root
    tables = [jnp.asarray((table * root).astype(jnp.bfloat16)) for table in dft_tables(fine, KEEP)]


    def sent(pieces, after):
        if after:
            pieces = lax.optimization_barrier((pieces, after))[0]
        others = {k: lax.ppermute(pieces[k], "tm", [(t, t ^ k) for t in range(n_time)]) for k in range(PEERS - 1, 0, -1)}
        return [pieces[0], *(others[k] for k in range(1, PEERS))]

    packed = [pack(voltages, place, 0, fine)]
    later = lax.optimization_barrier((place, packed[0]))[0]
    packed += [pack(voltages, later, h, fine) for h in range(1, chunks)]
    moved = [sent(packed[0], [])]
    moved.append(sent(packed[1], []))
    received = []
    for h in range(chunks):
        if h >= 2:
            moved[h][0], received[h - 2] = lax.optimization_barrier((moved[h][0], received[h - 2]))
        if h == 0:
            moved[0][0], packed = lax.optimization_barrier((moved[0][0], packed))
        mine = spectra(moved[h], place, taps, tables, frames, dests, chan)
        if h + 2 < chunks:
            moved.append(sent(packed[h + 2], [mine]))
        if h + 1 < chunks:
            mine, moved[h + 1][1:] = lax.optimization_barrier((mine, moved[h + 1][1:]))
        if received:
            mine, received[-1] = lax.optimization_barrier((mine, received[-1]))
        received.append(lax.all_to_all(mine, ("tm", "inp"), split_axis=0, concat_axis=0, tiled=True))
    ordered = [sort(array, 0, planes, n_group, own, past, chan) for array in received[:-1]]
    first = gram(ordered, chunks, n_group, scale)
    return gram(ordered, chunks, n_group, scale, first, received[-1], (planes, n_group, own, past, chan))


def solution(mesh):
    return jax.shard_map(
        per_device,
        mesh=mesh,
        in_specs=(P(None, "tm", "inp"), P()),
        out_specs=P(("tm", "inp"), None, None),
        check_vma=False,
    )
```
